512 devices in a mesh: row: 16 (over x, y), col: 32 (over z, core).
Axes of the slice: x: 4, y: 4, z: 16, core: 2. Of those that a mesh axis runs over, the one named last changes fastest.
Arguments:
- trailing: float32 [4096, 4096], P('row', 'col'), may hold values from -6 to 6
- panel_block: float32 [4096, 1024], P('row', 'col'), may hold values from -1.2 to 1.2
- inverse: float32 [1024, 1024], P(None, 'col'), may hold values from -1 to 1.5, as said below
- checksum: float32 [4096, 128], P('row', 'col'), may hold values from -24 to 24
Outputs:
- updated: float32 [4096, 4096], P('row', 'col')
- checksum_new: float32 [4096, 128], P('row', 'col')
- reencoded: float32 [4096, 128], P('row', 'col')
The draws below stay inside these ranges and needn't reach their ends.
Inputs may be any that keep to these rules, and one draw needn't show every extreme that they name: `inverse`: zero above the diagonal; the diagonal lies between 0.5 and 1.5.
All inputs are finite; a program needn't handle non-finite values.
Results may differ from the reference program's by a relative error of at most 0.00007.
Values sent between devices are 32-bit elements; how exact they have to be, the bound alone decides.
A program may use at most 64 MiB of HBM per device.

```python
import jax
import jax.numpy as jnp
from jax import lax

NB = 1024
ROW_DEV = 256
TRAIL = 4096
COL_DEV = 128
N_ROW = 16


def draw_inverse(key, part):
    first_key, second_key = jax.random.split(key)
    row_index = jnp.arange(NB)[:, None]
    column_index = jnp.arange(NB)[None, :]
    below = jax.random.normal(first_key, (NB, NB), jnp.float32) * (0.6 / NB ** 0.5)
    diagonal = jax.random.uniform(second_key, (NB,), jnp.float32, 0.5, 1.5)
    return jnp.where(row_index > column_index, below, jnp.where(row_index == column_index, diagonal[:, None], 0.0))


def block_levels(stream_key, extent, cuts, low, top_value):
    def one(dim, parts):
        steps = jax.random.uniform(jax.random.fold_in(jax.random.fold_in(stream_key, 6), dim), (parts,), jnp.float32, low / len(cuts), top_value / len(cuts))
        return jnp.repeat(jnp.exp(steps), extent[dim] // parts).reshape((-1,) + (1,) * (len(extent) - dim - 1))

    level = one(*cuts[0])
    for cut in cuts[1:]:
        level = level * one(*cut)
    return level


def gaussian(own_key, extent, deviation, reach, cuts=(), dtype=jnp.bfloat16):
    array = deviation * jax.random.normal(own_key, extent, jnp.float32)
    if cuts:
        array = array * block_levels(own_key, extent, cuts, -0.22, 0.18)
    return jnp.clip(array, -reach, reach).astype(dtype)


def setup_inputs(seed: int = 0) -> dict:
    key_of = jax.random.split(jax.random.key(seed), 5)
    trailing = gaussian(key_of[0], (TRAIL, TRAIL), 1.0, 6.0, ((0, 16), (1, 32)), jnp.float32)
    panel_block = gaussian(key_of[1], (TRAIL, NB), 0.18, 1.2, ((0, 16), (1, 32)), jnp.float32)
    inverse = draw_inverse(jax.random.fold_in(key_of[4], 71), 0)
    checksum = gaussian(key_of[3], (TRAIL, COL_DEV), 4.0, 24.0, ((0, 16), (1, 32)), jnp.float32)
    return dict(trailing=trailing, panel_block=panel_block, inverse=inverse, checksum=checksum)


def times_transpose(first_matrix, second_matrix):
    return lax.dot_general(first_matrix, second_matrix, (((1,), (1,)), ((), ())), precision=lax.Precision.HIGHEST, preferred_element_type=jnp.float32)


def reference(trailing, panel_block, inverse, checksum):
    factor_panel = times_transpose(panel_block, inverse)

    def update_rows(pieces):
        stored_rows, factor_rows = pieces
        return stored_rows - times_transpose(factor_rows, factor_panel)

    updated = lax.map(update_rows, (trailing.reshape(N_ROW, ROW_DEV, TRAIL), factor_panel.reshape(N_ROW, ROW_DEV, NB))).reshape(TRAIL, TRAIL)
    block_sum = jnp.sum(factor_panel.reshape(TRAIL // COL_DEV, COL_DEV, NB), axis=0)
    checksum_new = checksum - times_transpose(factor_panel, block_sum)
    reencoded = jnp.sum(updated.reshape(TRAIL, TRAIL // COL_DEV, COL_DEV), axis=1)
    return updated, checksum_new, reencoded
```

```python
import jax
import jax.numpy as jnp
from jax import lax
from jax.experimental import pallas as pl
from jax.experimental.pallas import tpu as pltpu
from jax.sharding import PartitionSpec as P

F32, BF16 = jnp.float32, jnp.bfloat16
MESH = pl.DeviceIdType.MESH
FIRST = (0, 1, 3, 6)


def remote(src, dst, send_sem, recv_sem, device):
    return pltpu.make_async_remote_copy(
        src_ref=src,
        dst_ref=dst,
        send_sem=send_sem,
        recv_sem=recv_sem,
        device_id=device,
        device_id_type=MESH,
    )


def arrived(ref, sem):
    pltpu.make_async_copy(ref, ref, sem).wait()


def split(value):
    high = value.astype(BF16)
    return high, (value - high.astype(F32)).astype(BF16)


def dot3(a, b, dims):
    def one(u, v):
        return lax.dot_general(u, v, (dims, ((), ())), preferred_element_type=F32)

    return one(a[0], b[0]) + (one(a[0], b[1]) + one(a[1], b[0]))


def kernel(
    t_ref, p_ref, i_ref, c_ref, u_out, c_out, e_out,
    inv, pr, pz, tt, tx, tr, lr, lz, ut, ux, ur, fin, fx,
    p_hi, p_lo, w_hi, w_lo, lr_hi, lr_lo, lc_hi, lc_lo,
    inv_s, inv_r, inv2_s, inv2_r, a_s, a_r, b_s, b_r, x_s, x_r, z_s, z_r, z2_s, z2_r,
    t_s, t_r, tr_s, tr_r, l_s, l_r, ur_s, ur_r,
):
    row, col = lax.axis_index("row"), lax.axis_index("col")
    z, k = col // 2, lax.rem(col, 2)
    x, y = row // 4, lax.rem(row, 4)
    q, w = z // 4, lax.rem(z, 4)
    p = lax.rem(y + w, 4)
    sibling = (row, 2 * z + 1 - k)
    half, other = pl.ds(pl.multiple_of(128 * k, 128), 128), pl.ds(pl.multiple_of(128 * (1 - k), 128), 128)

    def along(d):
        return (row, 2 * lax.rem(z + d + 16, 16) + k)

    barrier = pltpu.get_barrier_semaphore()

    @pl.loop(1, 32)
    def _(d):
        pl.semaphore_signal(barrier, inc=1, device_id=(row, lax.rem(col + d, 32)), device_id_type=MESH)

    @pl.loop(1, 16)
    def _(d):
        pl.semaphore_signal(barrier, inc=1, device_id=(lax.rem(row + d, 16), col), device_id_type=MESH)

    @pl.when(row != z)
    def _():
        pl.semaphore_signal(barrier, inc=1, device_id=(z, 2 * row + k), device_id_type=MESH)

    pl.semaphore_wait(barrier, jnp.where(row != z, 47, 46))

    def to_transposed():
        return remote(p_ref, pz.at[k, z], z_s, z_r, (z, 2 * row + k))

    @pl.when(row != z)
    def _():
        to_transposed().start()

    @pl.when(row == z)
    def _():
        pltpu.make_async_copy(p_ref, pz.at[k, z], z_r).start()

    def stride4(d):
        return remote(p_ref, pr.at[w, k, q], a_s.at[d], a_r, along(4 * d))

    for d in (2, 1, 3):
        stride4(d).start()
    pltpu.make_async_copy(p_ref, pr.at[w, k, q], a_r).start()

    tile_rows = pl.ds(pl.multiple_of(8 * x, 8), 8)
    slot = p * (p + 1) // 2 + q

    def piece(d):
        to = lax.rem(col + d, 32)
        columns = pl.ds(pl.multiple_of(128 * (2 * p + lax.rem(to, 2)), 128), 128)
        return i_ref.at[tile_rows, columns], to

    def send_piece(d):
        src, to = piece(d)
        return remote(src, inv.at[row, slot, k], inv_s.at[d], inv_r, (row, to))

    @pl.when(p >= q)
    def _():
        @pl.loop(1, 32)
        def _(d):
            send_piece(d).start()

        src, _ = piece(0)
        pltpu.make_async_copy(src, inv.at[row, slot, k], inv_r).start()

    tt[...] = t_ref[...].T

    def share(buf, into, i):
        return remote(buf.at[:, other], into, t_s.at[i], t_r.at[i], sibling)

    share(tt, tx, 0).start()

    arrived(pz.at[k, row], z_r)

    def panel_plane(d):
        return remote(pz.at[k, row], pz.at[k, row], z2_s.at[d], z2_r, (lax.rem(row + d, 16), col))

    @pl.loop(1, 16)
    def _(d):
        panel_plane(d).start()

    arrived(pr.at[w, k], a_r)
    first_two, last_two = pr.at[w, k, pl.ds(0, 2)], pr.at[w, k, pl.ds(2, 2)]
    group = [
        remote(pr.at[w, k], pr.at[w, k], b_s.at[0], b_r.at[0], along(1)),
        remote(pr.at[w, k], pr.at[w, k], b_s.at[1], b_r.at[1], along(-1)),
        remote(first_two, first_two, b_s.at[2], b_r.at[2], along(2)),
        remote(last_two, last_two, b_s.at[3], b_r.at[3], along(-2)),
    ]
    for g in group:
        g.start()

    def swap(i, v):
        return remote(pr.at[v, k], pr.at[v, k], x_s.at[i], x_r.at[i], sibling)

    swap(0, w).start()

    arrived(inv.at[row], inv_r)

    def inv_plane(d):
        return remote(inv.at[row], inv.at[row], inv2_s.at[d], inv2_r, (lax.rem(row + d, 16), col))

    @pl.loop(1, 16)
    def _(d):
        inv_plane(d).start()

    def send_sums(buf, into, send_sem, recv_sem):
        def make(d):
            to = lax.rem(z + d, 16)
            return remote(buf.at[pl.ds(pl.multiple_of(8 * to, 8), 8), half], into.at[z], send_sem.at[d], recv_sem, (row, 2 * to + k))

        return make

    def start_sums(buf, other_half, into, i, send_sem, recv_sem):
        share(buf, other_half, i).wait()
        buf[:, half] += other_half[...]
        make = send_sums(buf, into, send_sem, recv_sem)

        @pl.loop(1, 16)
        def _(d):
            make(d).start()

        into[z] = buf[pl.ds(pl.multiple_of(8 * z, 8), 8), half]

    start_sums(tt, tx, tr, 0, tr_s, tr_r)

    left, right, far = lax.rem(w + 3, 4), lax.rem(w + 1, 4), lax.rem(w + 2, 4)
    arrived(pr.at[left, k], b_r.at[0])
    swap(1, left).start()
    arrived(pr.at[right, k], b_r.at[1])
    swap(2, right).start()
    arrived(first_two, b_r.at[2])
    arrived(last_two, b_r.at[3])
    swap(3, far).start()

    arrived(pz.at[k, pl.ds(0, 15)], z2_r)
    swap_z = remote(pz.at[k], pz.at[k], x_s.at[4], x_r.at[4], sibling)
    swap_z.start()

    for i, v in enumerate((w, left, right, far)):
        arrived(pr.at[v, 1 - k], x_r.at[i])
    for i, v in enumerate((w, left, right, far)):
        swap(i, v).wait_send()
    for v in range(4):
        for h in range(2):
            for g in range(4):
                at = 32 * (2 * (4 * g + v) + h)
                high, low = split(pr[v, h, g])
                p_hi[at : at + 32, 0:256] = high
                p_lo[at : at + 32, 0:256] = low
    arrived(pz.at[1 - k], x_r.at[4])
    for h in range(2):
        for g in range(16):
            at = 32 * (2 * g + h)
            high, low = split(pz[h, g])
            p_hi[at : at + 32, 256:512] = high
            p_lo[at : at + 32, 256:512] = low

    arrived(inv.at[pl.ds(0, 15)], inv2_r)

    def give(n):
        return (
            remote(lr.at[n], lr.at[n], l_s.at[0, n // 2], l_r.at[0, n // 2], sibling),
            remote(lz.at[n, other], lz.at[n, other], l_s.at[1, n // 2], l_r.at[1, n // 2], sibling),
        )

    for b in range(4):
        depth = 256 * (b + 1)
        for g in range(b + 1):
            for v in range(4):
                source_y = (b - v) % 4
                for h in range(2):
                    at = 64 * (4 * g + v) + 32 * h
                    for pair in range(2):
                        both = jnp.concatenate(
                            [inv[4 * (2 * pair + e) + source_y, FIRST[b] + g, h] for e in range(2)], axis=0
                        )
                        high, low = split(both)
                        w_hi[b, at + 16 * pair : at + 16 * pair + 16, :] = high
                        w_lo[b, at + 16 * pair : at + 16 * pair + 16, :] = low
        block = dot3(
            (p_hi[0:depth, :], p_lo[0:depth, :]),
            (w_hi[b, 0:depth, :], w_lo[b, 0:depth, :]),
            ((0,), (0,)),
        )
        n = 2 * b + k
        lr[n] = block[0:256]
        lz[n] = block[256:512]
        for g in give(n):
            g.start()

    for b in range(4):
        n = 2 * b + 1 - k
        arrived(lr.at[n], l_r.at[0, b])
        arrived(lz.at[n, half], l_r.at[1, b])
    for n in range(8):
        at = slice(128 * n, 128 * n + 128)
        lr_hi[:, at], lr_lo[:, at] = split(lr[n])
        lc_hi[:, at], lc_lo[:, at] = split(lz[n, half])
    product = dot3((lr_hi[...], lr_lo[...]), (lc_hi[...], lc_lo[...]), ((1,), (1,)))
    ut[...] = product.T
    share(ut, ux, 1).start()
    u_out[...] = t_ref[...] - product
    start_sums(ut, ux, ur, 1, ur_s, ur_r)
    arrived(tr.at[pl.ds(0, 15)], tr_r)
    fin[0] = jnp.sum(tr[...], axis=0)
    arrived(ur.at[pl.ds(0, 15)], ur_r)
    fin[1] = jnp.sum(ur[...], axis=0)
    last = remote(fin, fx, t_s.at[2], t_r.at[2], sibling)
    last.start()
    last.wait()
    even = k == 0
    mine, theirs = fin[...], fx[...]
    sums = jnp.concatenate([jnp.where(even, mine, theirs), jnp.where(even, theirs, mine)], axis=2)
    sums = jnp.where(even, sums[:, 0:4], sums[:, 4:8])
    c_out[...] = c_ref[...] - sums[1]
    e_out[...] = sums[0] - sums[1]

    @pl.when(row != z)
    def _():
        to_transposed().wait_send()

    for d in (1, 2, 3):
        stride4(d).wait_send()

    @pl.when(p >= q)
    def _():
        @pl.loop(1, 32)
        def _(d):
            send_piece(d).wait_send()

    for g in group:
        g.wait_send()
    swap_z.wait_send()
    for b in range(4):
        for g in give(2 * b + k):
            g.wait_send()

    @pl.loop(1, 16)
    def _(d):
        panel_plane(d).wait_send()
        inv_plane(d).wait_send()
        send_sums(tt, tr, tr_s, tr_r)(d).wait_send()
        send_sums(ut, ur, ur_s, ur_r)(d).wait_send()


def on_device(trailing, panel_block, inverse, checksum):
    vmem = pl.BlockSpec(memory_space=pltpu.VMEM)
    dma = pltpu.SemaphoreType.DMA
    updated, checksum_new, reencoded = pl.pallas_call(
        kernel,
        out_shape=(
            jax.ShapeDtypeStruct((256, 128), F32),
            jax.ShapeDtypeStruct((4, 256), F32),
            jax.ShapeDtypeStruct((4, 256), F32),
        ),
        in_specs=[vmem] * 4,
        out_specs=(vmem,) * 3,
        scratch_shapes=[
            pltpu.VMEM((16, 10, 2, 8, 128), F32),
            pltpu.VMEM((4, 2, 4, 32, 256), F32),
            pltpu.VMEM((2, 16, 32, 256), F32),
            pltpu.VMEM((128, 256), F32),
            pltpu.VMEM((128, 128), F32),
            pltpu.VMEM((16, 8, 128), F32),
            pltpu.VMEM((8, 256, 128), F32),
            pltpu.VMEM((8, 256, 128), F32),
            pltpu.VMEM((128, 256), F32),
            pltpu.VMEM((128, 128), F32),
            pltpu.VMEM((16, 8, 128), F32),
            pltpu.VMEM((2, 8, 128), F32),
            pltpu.VMEM((2, 8, 128), F32),
            pltpu.VMEM((1024, 512), BF16),
            pltpu.VMEM((1024, 512), BF16),
            pltpu.VMEM((4, 1024, 128), BF16),
            pltpu.VMEM((4, 1024, 128), BF16),
            pltpu.VMEM((256, 1024), BF16),
            pltpu.VMEM((256, 1024), BF16),
            pltpu.VMEM((128, 1024), BF16),
            pltpu.VMEM((128, 1024), BF16),
            dma((32,)), dma, dma((16,)), dma,
            dma((4,)), dma, dma((4,)), dma((4,)),
            dma((5,)), dma((5,)), dma, dma, dma((16,)), dma,
            dma((3,)), dma((3,)), dma((16,)), dma,
            dma((2, 4)), dma((2, 4)), dma((16,)), dma,
        ],
        compiler_params=pltpu.CompilerParams(
            collective_id=0, has_side_effects=True, vmem_limit_bytes=32 * 1024 * 1024
        ),
    )(trailing, panel_block.T, inverse.T, checksum.T)
    return updated, checksum_new.T, reencoded.T


def solution(mesh):
    in_specs = (P("row", "col"), P("row", "col"), P(None, "col"), P("row", "col"))
    out_specs = (P("row", "col"), P("row", "col"), P("row", "col"))
    return jax.shard_map(
        on_device, mesh=mesh, in_specs=in_specs, out_specs=out_specs, check_vma=False
    )
```

```python
import jax
import jax.numpy as jnp
from jax import lax
from jax.experimental import pallas as pl
from jax.experimental.pallas import tpu as pltpu
from jax.sharding import PartitionSpec as P

F32, BF16 = jnp.float32, jnp.bfloat16
MESH = pl.DeviceIdType.MESH
FIRST = (0, 1, 3, 6)


def remote(src, dst, send_sem, recv_sem, device):
    return pltpu.make_async_remote_copy(
        src_ref=src,
        dst_ref=dst,
        send_sem=send_sem,
        recv_sem=recv_sem,
        device_id=device,
        device_id_type=MESH,
    )


def arrived(ref, sem):
    pltpu.make_async_copy(ref, ref, sem).wait()


def split(value):
    high = value.astype(BF16)
    return high, (value - high.astype(F32)).astype(BF16)


def dot3(a, b, dims):
    def one(u, v):
        return lax.dot_general(u, v, (dims, ((), ())), preferred_element_type=F32)

    return one(a[0], b[0]) + (one(a[0], b[1]) + one(a[1], b[0]))


def kernel(
    t_ref, p_ref, i_ref, c_ref, u_out, c_out, e_out,
    tv, pv, iv, cv, inv, pr, pz, p2, ps1, ps2, ps, tt, tx, tr, fin, fx, gb, rb,
    p_hi, p_lo, w_hi, w_lo, lr_hi, lr_lo, lc_hi, lc_lo,
    in_s, inv_s, inv_r, near_s, near_r, far_s, far_r, a_s, a_r, b_s, b_r, x_s, x_r,
    z_s, z_r, z2_s, z2_r, p1_s, p1_r, p3_s, p3_r, p4_s, p4_r, t_s, t_r, tr_s, tr_r, l_s, l_r,
):
    loads = [
        pltpu.make_async_copy(i_ref, iv, in_s.at[0]),
        pltpu.make_async_copy(p_ref, pv, in_s.at[1]),
        pltpu.make_async_copy(t_ref, tv, in_s.at[2]),
        pltpu.make_async_copy(c_ref, cv, in_s.at[3]),
    ]
    for load in loads:
        load.start()
    row, col = lax.axis_index("row"), lax.axis_index("col")
    z, k = col // 2, lax.rem(col, 2)
    x, y = row // 4, lax.rem(row, 4)
    q, w = z // 4, lax.rem(z, 4)
    p = lax.rem(y + w, 4)
    even = k == 0
    sibling = (row, 2 * z + 1 - k)
    half, other = pl.ds(pl.multiple_of(128 * k, 128), 128), pl.ds(pl.multiple_of(128 * (1 - k), 128), 128)

    def along(d):
        return (row, 2 * lax.rem(z + d + 16, 16) + k)

    barrier = pltpu.get_barrier_semaphore()

    @pl.loop(1, 32)
    def _(d):
        pl.semaphore_signal(barrier, inc=1, device_id=(row, lax.rem(col + d, 32)), device_id_type=MESH)

    @pl.loop(1, 16)
    def _(d):
        pl.semaphore_signal(barrier, inc=1, device_id=(lax.rem(row + d, 16), col), device_id_type=MESH)

    @pl.when(row != z)
    def _():
        pl.semaphore_signal(barrier, inc=1, device_id=(z, 2 * row + k), device_id_type=MESH)

    loads[1].wait()
    p2[...] = jnp.zeros_like(p2)
    p2[:, 0:32] = (pv[:, 0:128] + pv[:, 128:256]).T
    loads[2].wait()
    tt[...] = tv[...].T
    for b in range(2):
        nothing = jnp.zeros((256, 128), BF16)
        w_hi[b, 512 * b + 256 : 512 * b + 512, 0:128] = nothing
        w_lo[b, 512 * b + 256 : 512 * b + 512, 0:128] = nothing
    loads[0].wait()
    loads[3].wait()
    pl.semaphore_wait(barrier, jnp.where(row != z, 47, 46))

    tile_rows = pl.ds(pl.multiple_of(8 * x, 8), 8)
    slot = p * (p + 1) // 2 + q
    outer, inner = jnp.where(even, y, x), jnp.where(even, x, y)

    def piece(d):
        to = lax.rem(col + d, 32)
        columns = pl.ds(pl.multiple_of(128 * (2 * p + lax.rem(to, 2)), 128), 128)
        return iv.at[tile_rows, columns], to

    def send_piece(d):
        src, to = piece(d)
        return remote(src, inv.at[k, outer, inner, slot], inv_s.at[d], inv_r.at[k], (row, to))

    @pl.when(p >= q)
    def _():
        @pl.loop(1, 32)
        def _(d):
            send_piece(d).start()

        src, _ = piece(0)
        pltpu.make_async_copy(src, inv.at[k, outer, inner, slot], inv_r.at[k]).start()

    def to_transposed():
        return remote(pv, pz.at[k, z], z_s, z_r, (z, 2 * row + k))

    @pl.when(row != z)
    def _():
        to_transposed().start()

    @pl.when(row == z)
    def _():
        pltpu.make_async_copy(pv, pz.at[k, z], z_r).start()

    def stride4(d):
        return remote(pv, pr.at[w, k, q], a_s.at[d], a_r, along(4 * d))

    for d in (2, 1, 3):
        stride4(d).start()
    pltpu.make_async_copy(pv, pr.at[w, k, q], a_r).start()

    def panel_sum(d):
        to = lax.rem(row + d, 16)
        return remote(p2.at[pl.ds(pl.multiple_of(8 * to, 8), 8)], ps1.at[row], p1_s.at[d], p1_r, (to, col))

    @pl.loop(1, 16)
    def _(d):
        panel_sum(d).start()

    ps1[row] = p2[pl.ds(pl.multiple_of(8 * row, 8), 8)]

    share = remote(tt.at[:, other], tx, t_s.at[0], t_r.at[0], sibling)
    share.start()

    place = ((y, x), (x, y))

    def device(h, o, i):
        return (4 * i + o if h == 0 else 4 * o + i, col)

    def near(h, d):
        o, i = place[h]
        ref = inv.at[h, o, i]
        return remote(ref, ref, near_s.at[h, d - 1], near_r.at[h, d - 1], device(h, o, lax.rem(i + d, 4)))

    def far(h, back, d):
        o, i = place[h]
        ref = inv.at[h, o, lax.rem(i + 4 - back, 4)]
        return remote(ref, ref, far_s.at[h, back, d - 1], far_r.at[h], device(h, lax.rem(o + d, 4), i))

    for h in range(2):
        o, i = place[h]
        arrived(inv.at[h, o, i], inv_r.at[h])
        for d in (2, 1, 3):
            near(h, d).start()
        for d in (2, 1, 3):
            far(h, 0, d).start()

    arrived(pz.at[k, row], z_r)

    def panel_plane(d):
        return remote(pz.at[k, row], pz.at[k, row], z2_s.at[d], z2_r, (lax.rem(row + d, 16), col))

    @pl.loop(1, 16)
    def _(d):
        panel_plane(d).start()

    arrived(ps1.at[pl.ds(0, 15)], p1_r)
    ps2[...] = jnp.sum(ps1[...], axis=0)

    def sum_transposed():
        return remote(ps2, ps.at[k, z], p3_s, p3_r, (z, 2 * row + k))

    @pl.when(row != z)
    def _():
        sum_transposed().start()

    @pl.when(row == z)
    def _():
        pltpu.make_async_copy(ps2, ps.at[k, z], p3_r).start()

    arrived(pr.at[w, k], a_r)
    first_two, last_two = pr.at[w, k, pl.ds(0, 2)], pr.at[w, k, pl.ds(2, 2)]
    group = [
        remote(first_two, first_two, b_s.at[2], b_r.at[2], along(2)),
        remote(last_two, last_two, b_s.at[3], b_r.at[3], along(-2)),
        remote(pr.at[w, k], pr.at[w, k], b_s.at[0], b_r.at[0], along(1)),
        remote(pr.at[w, k], pr.at[w, k], b_s.at[1], b_r.at[1], along(-1)),
    ]
    for g in group:
        g.start()

    def swap(i, v):
        return remote(pr.at[v, k], pr.at[v, k], x_s.at[i], x_r.at[i], sibling)

    swap(0, w).start()

    for d in (1, 3, 2):
        for h in range(2):
            o, i = place[h]
            arrived(inv.at[h, o, lax.rem(i + 4 - d, 4)], near_r.at[h, d - 1])
            for e in (2, 1, 3):
                far(h, d, e).start()

    arrived(ps.at[k, row], p3_r)

    def sum_plane(d):
        return remote(ps.at[k, row], ps.at[k, row], p4_s.at[d], p4_r, (lax.rem(row + d, 16), col))

    @pl.loop(1, 16)
    def _(d):
        sum_plane(d).start()

    share.wait()
    tt[:, half] += tx[...]

    def block_sum(d):
        to = lax.rem(z + d, 16)
        return remote(tt.at[pl.ds(pl.multiple_of(8 * to, 8), 8), half], tr.at[z], tr_s.at[d], tr_r, (row, 2 * to + k))

    @pl.loop(1, 16)
    def _(d):
        block_sum(d).start()

    tr[z] = tt[pl.ds(pl.multiple_of(8 * z, 8), 8), half]

    left, right, across = lax.rem(w + 3, 4), lax.rem(w + 1, 4), lax.rem(w + 2, 4)
    arrived(pr.at[left, k], b_r.at[0])
    swap(1, left).start()
    arrived(pr.at[right, k], b_r.at[1])
    swap(2, right).start()
    arrived(first_two, b_r.at[2])
    arrived(last_two, b_r.at[3])
    swap(3, across).start()

    arrived(pz.at[k, pl.ds(0, 15)], z2_r)
    swap_z = remote(pz.at[k], pz.at[k], x_s.at[4], x_r.at[4], sibling)
    swap_z.start()
    arrived(ps.at[k, pl.ds(0, 15)], p4_r)
    swap_s = remote(ps.at[k], ps.at[k], x_s.at[5], x_r.at[5], sibling)
    swap_s.start()

    for i, v in enumerate((w, left, right, across)):
        arrived(pr.at[v, 1 - k], x_r.at[i])
    for i, v in enumerate((w, left, right, across)):
        swap(i, v).wait_send()
    for m in range(8):
        parts = [pr[2 * (m % 2) + e // 2, e % 2, m // 2] for e in range(4)]
        at = slice(128 * m, 128 * m + 128)
        p_hi[0:256, at], p_lo[0:256, at] = split(jnp.concatenate(parts, axis=0).T)
    arrived(pz.at[1 - k], x_r.at[4])
    for m in range(8):
        parts = [pz[e % 2, 2 * m + e // 2] for e in range(4)]
        at = slice(128 * m, 128 * m + 128)
        p_hi[256:512, at], p_lo[256:512, at] = split(jnp.concatenate(parts, axis=0).T)
    arrived(ps.at[1 - k], x_r.at[5])
    for m in range(8):
        parts = jnp.concatenate([ps[e % 2, 2 * m + e // 2][:, 0:32] for e in range(4)], axis=1)
        at = slice(128 * m, 128 * m + 128)
        p_hi[512:528, at], p_lo[512:528, at] = split(jnp.concatenate([parts, jnp.zeros_like(parts)], axis=0))

    arrived(tr.at[pl.ds(0, 15)], tr_r)
    fin[...] = jnp.sum(tr[...], axis=0)
    last = remote(fin, fx, t_s.at[1], t_r.at[1], sibling)
    last.start()

    for h in range(2):
        arrived(inv.at[h, pl.ds(0, 3)], far_r.at[h])

    def put(at, rows, c_rows, s_rows):
        lr_hi[:, at], lr_lo[:, at] = split(rows)
        high, low = split(jnp.concatenate([c_rows, s_rows, jnp.zeros_like(s_rows)], axis=0))
        lc_hi[:, at], lc_lo[:, at] = high, low

    def give(b):
        return remote(gb.at[b], rb.at[b], l_s.at[b], l_r.at[b], sibling)

    for b in range(2):
        depth = 512 * (b + 1)
        for e in range(2):
            n = 2 * b + e
            for g in range(n + 1):
                for v in range(4):
                    sy = (n - v) % 4
                    for h in range(2):
                        at = 64 * (4 * g + v) + 32 * h
                        tiles = [inv[h, sy, sx, FIRST[n] + g] if h == 0 else inv[h, sx, sy, FIRST[n] + g] for sx in range(4)]
                        high, low = split(jnp.concatenate(tiles, axis=0))
                        w_hi[b, at : at + 32, 128 * e : 128 * e + 128] = high
                        w_lo[b, at : at + 32, 128 * e : 128 * e + 128] = low
        block = dot3(
            (p_hi[:, 0:depth], p_lo[:, 0:depth]),
            (w_hi[b, 0:depth, :], w_lo[b, 0:depth, :]),
            ((1,), (0,)),
        )
        one, two = block[256:384], block[384:512]
        gb[b, 0:256] = block[0:256]
        gb[b, 256:384] = jnp.where(even, two, one)
        gb[b, 384:392] = block[512:520]
        give(b).start()
        put(slice(512 * b, 512 * b + 256), block[0:256], jnp.where(even, one, two), block[512:520])

    for b in range(2):
        arrived(rb.at[b], l_r.at[b])
        put(slice(512 * b + 256, 512 * b + 512), rb[b, 0:256], rb[b, 256:384], rb[b, 384:392])
    product = dot3((lr_hi[...], lr_lo[...]), (lc_hi[...], lc_lo[...]), ((1,), (1,)))
    u_out[...] = tv[...] - product[:, 0:128]
    correction = product[:, 128:136].T
    correction = jnp.where(even, correction[0:4], correction[4:8])
    last.wait()
    mine, theirs = fin[...], fx[...]
    sums = jnp.concatenate([jnp.where(even, mine, theirs), jnp.where(even, theirs, mine)], axis=1)
    c_out[...] = cv[...] - correction
    e_out[...] = jnp.where(even, sums[0:4], sums[4:8]) - correction

    @pl.when(row != z)
    def _():
        to_transposed().wait_send()
        sum_transposed().wait_send()

    for d in (1, 2, 3):
        stride4(d).wait_send()

    @pl.when(p >= q)
    def _():
        @pl.loop(1, 32)
        def _(d):
            send_piece(d).wait_send()

    for g in group:
        g.wait_send()
    swap_z.wait_send()
    swap_s.wait_send()
    for b in range(2):
        give(b).wait_send()
    for h in range(2):
        for d in (1, 2, 3):
            near(h, d).wait_send()
            for back in range(4):
                far(h, back, d).wait_send()

    @pl.loop(1, 16)
    def _(d):
        panel_plane(d).wait_send()
        panel_sum(d).wait_send()
        sum_plane(d).wait_send()
        block_sum(d).wait_send()


def on_device(trailing, panel_block, inverse, checksum):
    vmem = pl.BlockSpec(memory_space=pltpu.VMEM)
    dma = pltpu.SemaphoreType.DMA
    updated, checksum_new, reencoded = pl.pallas_call(
        kernel,
        out_shape=(
            jax.ShapeDtypeStruct((256, 128), F32),
            jax.ShapeDtypeStruct((4, 256), F32),
            jax.ShapeDtypeStruct((4, 256), F32),
        ),
        in_specs=[pl.BlockSpec(memory_space=pltpu.HBM)] * 4,
        out_specs=(vmem,) * 3,
        scratch_shapes=[
            pltpu.VMEM((256, 128), F32),
            pltpu.VMEM((32, 256), F32),
            pltpu.VMEM((32, 1024), F32),
            pltpu.VMEM((4, 256), F32),
            pltpu.VMEM((2, 4, 4, 10, 8, 128), F32),
            pltpu.VMEM((4, 2, 4, 32, 256), F32),
            pltpu.VMEM((2, 16, 32, 256), F32),
            pltpu.VMEM((128, 128), F32),
            pltpu.VMEM((16, 8, 128), F32),
            pltpu.VMEM((8, 128), F32),
            pltpu.VMEM((2, 16, 8, 128), F32),
            pltpu.VMEM((128, 256), F32),
            pltpu.VMEM((128, 128), F32),
            pltpu.VMEM((16, 8, 128), F32),
            pltpu.VMEM((8, 128), F32),
            pltpu.VMEM((8, 128), F32),
            pltpu.VMEM((2, 392, 256), F32),
            pltpu.VMEM((2, 392, 256), F32),
            pltpu.VMEM((528, 1024), BF16),
            pltpu.VMEM((528, 1024), BF16),
            pltpu.VMEM((2, 1024, 256), BF16),
            pltpu.VMEM((2, 1024, 256), BF16),
            pltpu.VMEM((256, 1024), BF16),
            pltpu.VMEM((256, 1024), BF16),
            pltpu.VMEM((144, 1024), BF16),
            pltpu.VMEM((144, 1024), BF16),
            dma((4,)), dma((32,)), dma((2,)), dma((2, 3)), dma((2, 3)), dma((2, 4, 3)), dma((2,)),
            dma((4,)), dma, dma((4,)), dma((4,)), dma((6,)), dma((6,)),
            dma, dma, dma((16,)), dma, dma((16,)), dma, dma, dma, dma((16,)), dma,
            dma((2,)), dma((2,)), dma((16,)), dma, dma((2,)), dma((2,)),
        ],
        compiler_params=pltpu.CompilerParams(
            collective_id=0, has_side_effects=True, vmem_limit_bytes=48 * 1024 * 1024
        ),
    )(trailing, panel_block.T, inverse.T, checksum.T)
    return updated, checksum_new.T, reencoded.T


def solution(mesh):
    in_specs = (P("row", "col"), P("row", "col"), P(None, "col"), P("row", "col"))
    out_specs = (P("row", "col"), P("row", "col"), P("row", "col"))
    return jax.shard_map(
        on_device, mesh=mesh, in_specs=in_specs, out_specs=out_specs, check_vma=False
    )
```

```python
import jax
import jax.numpy as jnp
from jax import lax
from jax.experimental import pallas as pl
from jax.experimental.pallas import tpu as pltpu
from jax.sharding import PartitionSpec as P

F32, BF16 = jnp.float32, jnp.bfloat16
MESH = pl.DeviceIdType.MESH
FIRST = (0, 1, 3, 6)


def remote(src, dst, send_sem, recv_sem, device):
    return pltpu.make_async_remote_copy(
        src_ref=src,
        dst_ref=dst,
        send_sem=send_sem,
        recv_sem=recv_sem,
        device_id=device,
        device_id_type=MESH,
    )


def arrived(ref, sem):
    pltpu.make_async_copy(ref, ref, sem).wait()


def split(value):
    high = value.astype(BF16)
    return high, (value - high.astype(F32)).astype(BF16)


def dot3(a, b, dims):
    def one(u, v):
        return lax.dot_general(u, v, (dims, ((), ())), preferred_element_type=F32)

    return one(a[0], b[0]) + (one(a[0], b[1]) + one(a[1], b[0]))


def kernel(
    t_ref, p_ref, i_ref, c_ref, u_out, c_out, e_out,
    tv, pv, cv, inv, pr, pz, p2, ps1, ps2, ps, tt, tx, tq, ta, tb, tc, fin, fx, gb, rb,
    p_hi, p_lo, w_hi, w_lo, lr_hi, lr_lo, lc_hi, lc_lo,
    in_s, near_s, near_r, far_s, far_r, a_s, a_r, b_s, b_r, x_s, x_r,
    z_s, z_r, z2_s, z2_r, p1_s, p1_r, p3_s, p3_r, p4_s, p4_r, t_s, t_r, ta_s, ta_r, tc_s, tc_r, l_s, l_r,
):
    row, col = lax.axis_index("row"), lax.axis_index("col")
    z, k = col // 2, lax.rem(col, 2)
    x, y = row // 4, lax.rem(row, 4)
    q, w = z // 4, lax.rem(z, 4)
    p = lax.rem(y + w, 4)
    even = k == 0
    tile_rows = pl.ds(pl.multiple_of(8 * x, 8), 8)
    loads = [
        pltpu.make_async_copy(p_ref, pv.at[pl.ds(0, 32)], in_s.at[0]),
        pltpu.make_async_copy(i_ref.at[tile_rows, pl.ds(pl.multiple_of(256 * p, 256), 256)], pv.at[pl.ds(32, 8)], in_s.at[1]),
        pltpu.make_async_copy(t_ref, tv, in_s.at[2]),
        pltpu.make_async_copy(c_ref, cv, in_s.at[3]),
    ]
    for load in loads:
        load.start()
    sibling = (row, 2 * z + 1 - k)
    half, other = pl.ds(pl.multiple_of(128 * k, 128), 128), pl.ds(pl.multiple_of(128 * (1 - k), 128), 128)

    def along(d):
        return (row, 2 * lax.rem(z + d + 16, 16) + k)

    barrier = pltpu.get_barrier_semaphore()

    for d in (8, 4, -4, 2, -2, 1, -1):
        pl.semaphore_signal(barrier, inc=1, device_id=along(d), device_id_type=MESH)
    pl.semaphore_signal(barrier, inc=1, device_id=sibling, device_id_type=MESH)

    @pl.loop(1, 16)
    def _(d):
        pl.semaphore_signal(barrier, inc=1, device_id=(lax.rem(row + d, 16), col), device_id_type=MESH)

    @pl.when(row != z)
    def _():
        pl.semaphore_signal(barrier, inc=1, device_id=(z, 2 * row + k), device_id_type=MESH)

    loads[0].wait()
    p2[...] = jnp.zeros_like(p2)
    p2[:, 0:32] = (pv[0:32, 0:128] + pv[0:32, 128:256]).T
    loads[2].wait()
    tt[...] = tv[...].T
    for b in range(2):
        nothing = jnp.zeros((256, 128), BF16)
        w_hi[b, 512 * b + 256 : 512 * b + 512, 0:128] = nothing
        w_lo[b, 512 * b + 256 : 512 * b + 512, 0:128] = nothing
    loads[1].wait()
    loads[3].wait()
    pl.semaphore_wait(barrier, jnp.where(row != z, 24, 23))

    def stride4(d):
        return remote(pv, pr.at[w, k, q], a_s.at[d], a_r.at[d], along(4 * d))

    def to_group(back):
        at = lax.rem(q + 4 - back, 4)
        src, dst = pr.at[w, k, at] if back else pv, pr.at[w, k, at]
        low = at < 2
        return [
            remote(src, dst, b_s.at[back, 2], b_r.at[jnp.where(low, 2, 3)], along(jnp.where(low, 2, -2))),
            remote(src, dst, b_s.at[back, 0], b_r.at[0], along(1)),
            remote(src, dst, b_s.at[back, 1], b_r.at[1], along(-1)),
        ]

    for d in (2, 1, 3):
        stride4(d).start()
    for g in to_group(0):
        g.start()
    pltpu.make_async_copy(pv, pr.at[w, k, q], a_r.at[0]).start()

    def to_transposed():
        return remote(pv.at[pl.ds(0, 32)], pz.at[k, z], z_s, z_r, (z, 2 * row + k))

    @pl.when(row != z)
    def _():
        to_transposed().start()

    @pl.when(row == z)
    def _():
        pltpu.make_async_copy(pv.at[pl.ds(0, 32)], pz.at[k, z], z_r).start()

    def panel_sum(d):
        to = lax.rem(row + d, 16)
        return remote(p2.at[pl.ds(pl.multiple_of(8 * to, 8), 8)], ps1.at[row], p1_s.at[d], p1_r, (to, col))

    @pl.loop(1, 16)
    def _(d):
        panel_sum(d).start()

    ps1[row] = p2[pl.ds(pl.multiple_of(8 * row, 8), 8)]

    share = remote(tt.at[:, other], tx, t_s.at[0], t_r.at[0], sibling)
    share.start()

    arrived(ps1.at[pl.ds(0, 15)], p1_r)
    ps2[...] = jnp.sum(ps1[...], axis=0)

    def sum_transposed():
        return remote(ps2, ps.at[k, z], p3_s, p3_r, (z, 2 * row + k))

    @pl.when(row != z)
    def _():
        sum_transposed().start()

    @pl.when(row == z)
    def _():
        pltpu.make_async_copy(ps2, ps.at[k, z], p3_r).start()

    for d in (1, 3, 2):
        arrived(pr.at[w, k, lax.rem(q + 4 - d, 4)], a_r.at[d])
        for g in to_group(d):
            g.start()
    arrived(pr.at[w, k, q], a_r.at[0])
    first_two, last_two = pr.at[w, k, pl.ds(0, 2)], pr.at[w, k, pl.ds(2, 2)]

    def swap(i, v):
        return remote(pr.at[v, k], pr.at[v, k], x_s.at[i], x_r.at[i], sibling)

    swap(0, w).start()

    arrived(pz.at[k, row], z_r)

    def panel_plane(d):
        return remote(pz.at[k, row], pz.at[k, row], z2_s.at[d], z2_r, (lax.rem(row + d, 16), col))

    @pl.loop(1, 16)
    def _(d):
        panel_plane(d).start()

    share.wait()
    tt[:, half] += tx[...]

    for d in range(16):
        tq[d % 4, d // 4] = tt[8 * d : 8 * d + 8, half]
    left, right, across = lax.rem(w + 3, 4), lax.rem(w + 1, 4), lax.rem(w + 2, 4)
    gather_sums = [
        remote(tq.at[left], ta.at[0], ta_s.at[0], ta_r.at[0], along(-1)),
        remote(tq.at[right], ta.at[1], ta_s.at[1], ta_r.at[1], along(1)),
        remote(tq.at[across, pl.ds(0, 2)], ta.at[2, pl.ds(0, 2)], ta_s.at[2], ta_r.at[2], along(2)),
        remote(tq.at[across, pl.ds(2, 2)], ta.at[2, pl.ds(2, 2)], ta_s.at[3], ta_r.at[3], along(-2)),
    ]
    for g in gather_sums:
        g.start()

    arrived(pr.at[left, k], b_r.at[0])
    swap(1, left).start()
    arrived(pr.at[right, k], b_r.at[1])
    swap(2, right).start()
    arrived(first_two, b_r.at[2])
    arrived(last_two, b_r.at[3])
    swap(3, across).start()

    place = ((y, x), (x, y))
    parity = (k, 1 - k)

    def device(h, o, i):
        return (4 * i + o if h == 0 else 4 * o + i, col)

    def near(h, d):
        o, i = place[h]
        ref = inv.at[h, o, i]
        return remote(ref, ref, near_s.at[h, d - 1], near_r.at[h, d - 1], device(h, o, lax.rem(i + d, 4)))

    def far(h, back, d):
        o, i = place[h]
        ref = inv.at[h, o, lax.rem(i + 4 - back, 4)]
        return remote(ref, ref, far_s.at[h, back, d - 1], far_r.at[h], device(h, lax.rem(o + d, 4), i))

    def pack(h):
        o, i = place[h]
        for n in range(4):
            for g in range(n + 1):
                inv[h, o, i, FIRST[n] + g] = pr[lax.rem(n + 4 - y, 4), parity[h], g, 32:40, half]
        for d in (2, 1, 3):
            near(h, d).start()
        for d in (2, 1, 3):
            far(h, 0, d).start()

    pack(0)
    arrived(ps.at[k, row], p3_r)

    def sum_plane(d):
        return remote(ps.at[k, row], ps.at[k, row], p4_s.at[d], p4_r, (lax.rem(row + d, 16), col))

    @pl.loop(1, 16)
    def _(d):
        sum_plane(d).start()

    for i, v in enumerate((w, left, right, across)):
        arrived(pr.at[v, 1 - k], x_r.at[i])
    pack(1)

    def forward(h, d):
        o, i = place[h]
        arrived(inv.at[h, o, lax.rem(i + 4 - d, 4)], near_r.at[h, d - 1])
        for e in (2, 1, 3):
            far(h, d, e).start()

    for d in (1, 3, 2):
        forward(0, d)
    for d in (1, 3, 2):
        forward(1, d)

    for i, g in enumerate(gather_sums):
        arrived((ta.at[i] if i < 2 else ta.at[2, pl.ds(2 * i - 4, 2)]), ta_r.at[i])
    tb[...] = tq[w] + ta[0] + ta[1] + ta[2]

    def block_sum(d):
        return remote(tb.at[lax.rem(q + d, 4)], tc.at[q], tc_s.at[d], tc_r, along(4 * d))

    for d in (2, 1, 3):
        block_sum(d).start()
    tc[q] = tb[q]

    arrived(pz.at[k, pl.ds(0, 15)], z2_r)
    swap_z = remote(pz.at[k], pz.at[k], x_s.at[4], x_r.at[4], sibling)
    swap_z.start()
    arrived(ps.at[k, pl.ds(0, 15)], p4_r)
    swap_s = remote(ps.at[k], ps.at[k], x_s.at[5], x_r.at[5], sibling)
    swap_s.start()

    for i, v in enumerate((w, left, right, across)):
        swap(i, v).wait_send()
    for m in range(8):
        parts = [pr[2 * (m % 2) + e // 2, parity[e % 2], m // 2, 0:32] for e in range(4)]
        at = slice(128 * m, 128 * m + 128)
        p_hi[0:256, at], p_lo[0:256, at] = split(jnp.concatenate(parts, axis=0).T)
    arrived(pz.at[1 - k], x_r.at[4])
    for m in range(8):
        parts = [pz[parity[e % 2], 2 * m + e // 2] for e in range(4)]
        at = slice(128 * m, 128 * m + 128)
        p_hi[256:512, at], p_lo[256:512, at] = split(jnp.concatenate(parts, axis=0).T)
    arrived(ps.at[1 - k], x_r.at[5])
    for m in range(8):
        parts = jnp.concatenate([ps[parity[e % 2], 2 * m + e // 2][:, 0:32] for e in range(4)], axis=1)
        at = slice(128 * m, 128 * m + 128)
        p_hi[512:528, at], p_lo[512:528, at] = split(jnp.concatenate([parts, jnp.zeros_like(parts)], axis=0))

    arrived(tc.at[pl.ds(0, 3)], tc_r)
    fin[...] = jnp.sum(tc[...], axis=0)
    last = remote(fin, fx, t_s.at[1], t_r.at[1], sibling)
    last.start()

    for h in range(2):
        arrived(inv.at[h, pl.ds(0, 3)], far_r.at[h])

    def put(at, rows, c_rows, s_rows):
        lr_hi[:, at], lr_lo[:, at] = split(rows)
        high, low = split(jnp.concatenate([c_rows, s_rows, jnp.zeros_like(s_rows)], axis=0))
        lc_hi[:, at], lc_lo[:, at] = high, low

    def give(b):
        return remote(gb.at[b], rb.at[b], l_s.at[b], l_r.at[b], sibling)

    for b in range(2):
        depth = 512 * (b + 1)
        for e in range(2):
            n = 2 * b + e
            for g in range(n + 1):
                for v in range(4):
                    sy = (n - v) % 4
                    for h in range(2):
                        at = 64 * (4 * g + v) + 32 * h
                        tiles = [inv[h, sy, sx, FIRST[n] + g] if h == 0 else inv[h, sx, sy, FIRST[n] + g] for sx in range(4)]
                        high, low = split(jnp.concatenate(tiles, axis=0))
                        w_hi[b, at : at + 32, 128 * e : 128 * e + 128] = high
                        w_lo[b, at : at + 32, 128 * e : 128 * e + 128] = low
        block = dot3(
            (p_hi[:, 0:depth], p_lo[:, 0:depth]),
            (w_hi[b, 0:depth, :], w_lo[b, 0:depth, :]),
            ((1,), (0,)),
        )
        one, two = block[256:384], block[384:512]
        gb[b, 0:256] = block[0:256]
        gb[b, 256:384] = jnp.where(even, two, one)
        gb[b, 384:392] = block[512:520]
        give(b).start()
        put(slice(512 * b, 512 * b + 256), block[0:256], jnp.where(even, one, two), block[512:520])

    for b in range(2):
        arrived(rb.at[b], l_r.at[b])
        put(slice(512 * b + 256, 512 * b + 512), rb[b, 0:256], rb[b, 256:384], rb[b, 384:392])
    product = dot3((lr_hi[...], lr_lo[...]), (lc_hi[...], lc_lo[...]), ((1,), (1,)))
    u_out[...] = tv[...] - product[:, 0:128]
    correction = product[:, 128:136].T
    correction = jnp.where(even, correction[0:4], correction[4:8])
    last.wait()
    mine, theirs = fin[...], fx[...]
    sums = jnp.concatenate([jnp.where(even, mine, theirs), jnp.where(even, theirs, mine)], axis=1)
    c_out[...] = cv[...] - correction
    e_out[...] = jnp.where(even, sums[0:4], sums[4:8]) - correction

    @pl.when(row != z)
    def _():
        to_transposed().wait_send()
        sum_transposed().wait_send()

    for d in (1, 2, 3):
        stride4(d).wait_send()
        block_sum(d).wait_send()

    for g in gather_sums + [g for back in range(4) for g in to_group(back)]:
        g.wait_send()
    swap_z.wait_send()
    swap_s.wait_send()
    for b in range(2):
        give(b).wait_send()
    for h in range(2):
        for d in (1, 2, 3):
            near(h, d).wait_send()
            for back in range(4):
                far(h, back, d).wait_send()

    @pl.loop(1, 16)
    def _(d):
        panel_plane(d).wait_send()
        panel_sum(d).wait_send()
        sum_plane(d).wait_send()


def on_device(trailing, panel_block, inverse, checksum):
    vmem = pl.BlockSpec(memory_space=pltpu.VMEM)
    dma = pltpu.SemaphoreType.DMA
    updated, checksum_new, reencoded = pl.pallas_call(
        kernel,
        out_shape=(
            jax.ShapeDtypeStruct((256, 128), F32),
            jax.ShapeDtypeStruct((4, 256), F32),
            jax.ShapeDtypeStruct((4, 256), F32),
        ),
        in_specs=[pl.BlockSpec(memory_space=pltpu.HBM)] * 4,
        out_specs=(vmem,) * 3,
        scratch_shapes=[
            pltpu.VMEM((256, 128), F32),
            pltpu.VMEM((40, 256), F32),
            pltpu.VMEM((4, 256), F32),
            pltpu.VMEM((2, 4, 4, 10, 8, 128), F32),
            pltpu.VMEM((4, 2, 4, 40, 256), F32),
            pltpu.VMEM((2, 16, 32, 256), F32),
            pltpu.VMEM((128, 128), F32),
            pltpu.VMEM((16, 8, 128), F32),
            pltpu.VMEM((8, 128), F32),
            pltpu.VMEM((2, 16, 8, 128), F32),
            pltpu.VMEM((128, 256), F32),
            pltpu.VMEM((128, 128), F32),
            pltpu.VMEM((4, 4, 8, 128), F32),
            pltpu.VMEM((3, 4, 8, 128), F32),
            pltpu.VMEM((4, 8, 128), F32),
            pltpu.VMEM((4, 8, 128), F32),
            pltpu.VMEM((8, 128), F32),
            pltpu.VMEM((8, 128), F32),
            pltpu.VMEM((2, 392, 256), F32),
            pltpu.VMEM((2, 392, 256), F32),
            pltpu.VMEM((528, 1024), BF16),
            pltpu.VMEM((528, 1024), BF16),
            pltpu.VMEM((2, 1024, 256), BF16),
            pltpu.VMEM((2, 1024, 256), BF16),
            pltpu.VMEM((256, 1024), BF16),
            pltpu.VMEM((256, 1024), BF16),
            pltpu.VMEM((144, 1024), BF16),
            pltpu.VMEM((144, 1024), BF16),
            dma((4,)), dma((2, 3)), dma((2, 3)), dma((2, 4, 3)), dma((2,)),
            dma((4,)), dma((4,)), dma((4, 3)), dma((4,)), dma((6,)), dma((6,)),
            dma, dma, dma((16,)), dma, dma((16,)), dma, dma, dma, dma((16,)), dma,
            dma((2,)), dma((2,)), dma((4,)), dma((4,)), dma((4,)), dma, dma((2,)), dma((2,)),
        ],
        compiler_params=pltpu.CompilerParams(
            collective_id=0, has_side_effects=True, vmem_limit_bytes=62 * 1024 * 1024
        ),
    )(trailing, panel_block.T, inverse.T, checksum.T)
    return updated, checksum_new.T, reencoded.T


def solution(mesh):
    in_specs = (P("row", "col"), P("row", "col"), P(None, "col"), P("row", "col"))
    out_specs = (P("row", "col"), P("row", "col"), P("row", "col"))
    return jax.shard_map(
        on_device, mesh=mesh, in_specs=in_specs, out_specs=out_specs, check_vma=False
    )
```

```python
import jax
import jax.numpy as jnp
from jax import lax
from jax.experimental import pallas as pl
from jax.experimental.pallas import tpu as pltpu
from jax.sharding import PartitionSpec as P

F32, BF16 = jnp.float32, jnp.bfloat16
MESH = pl.DeviceIdType.MESH
FIRST = (0, 1, 3, 6)


def remote(src, dst, send_sem, recv_sem, device):
    return pltpu.make_async_remote_copy(
        src_ref=src,
        dst_ref=dst,
        send_sem=send_sem,
        recv_sem=recv_sem,
        device_id=device,
        device_id_type=MESH,
    )


def arrived(ref, sem):
    pltpu.make_async_copy(ref, ref, sem).wait()


def split(value):
    high = value.astype(BF16)
    return high, (value - high.astype(F32)).astype(BF16)


def dot3(a, b, dims):
    def one(u, v):
        return lax.dot_general(u, v, (dims, ((), ())), preferred_element_type=F32)

    return one(a[0], b[0]) + (one(a[0], b[1]) + one(a[1], b[0]))


def kernel(
    t_ref, p_ref, i_ref, c_ref, u_out, c_out, e_out,
    tv, pv, cv, inv, pr, pz, p2, ps1, ps2, ps, tt, tx, tq, ta, tb, tc, fin, fx, gb, rb, part_0,
    p_hi, p_lo, w_hi, w_lo, lr_hi, lr_lo, lc_hi, lc_lo,
    in_s, near_s, near_r, far_s, far_r, a_s, a_r, b_s, b_r, x_s, x_r,
    z_s, z_r, z2_s, z2_r, p1_s, p1_r, p3_s, p3_r, p4_s, p4_r, t_s, t_r, ta_s, ta_r, tc_s, tc_r, l_s, l_r,
):
    row, col = lax.axis_index("row"), lax.axis_index("col")
    z, k = col // 2, lax.rem(col, 2)
    x, y = row // 4, lax.rem(row, 4)
    q, w = z // 4, lax.rem(z, 4)
    p = lax.rem(y + w, 4)
    even = k == 0
    tile_rows = pl.ds(pl.multiple_of(8 * x, 8), 8)
    loads = [
        pltpu.make_async_copy(p_ref, pv.at[pl.ds(0, 32)], in_s.at[0]),
        pltpu.make_async_copy(i_ref.at[tile_rows, pl.ds(pl.multiple_of(256 * p, 256), 256)], pv.at[pl.ds(32, 8)], in_s.at[1]),
        pltpu.make_async_copy(t_ref, tv, in_s.at[2]),
        pltpu.make_async_copy(c_ref, cv, in_s.at[3]),
    ]
    for load in loads:
        load.start()
    sibling = (row, 2 * z + 1 - k)
    half, other = pl.ds(pl.multiple_of(128 * k, 128), 128), pl.ds(pl.multiple_of(128 * (1 - k), 128), 128)

    def along(d):
        return (row, 2 * lax.rem(z + d + 16, 16) + k)

    barrier = pltpu.get_barrier_semaphore()

    for d in (8, 4, -4, 2, -2, 1, -1):
        pl.semaphore_signal(barrier, inc=1, device_id=along(d), device_id_type=MESH)
    pl.semaphore_signal(barrier, inc=1, device_id=sibling, device_id_type=MESH)

    @pl.loop(1, 16)
    def _(d):
        pl.semaphore_signal(barrier, inc=1, device_id=(lax.rem(row + d, 16), col), device_id_type=MESH)

    @pl.when(row != z)
    def _():
        pl.semaphore_signal(barrier, inc=1, device_id=(z, 2 * row + k), device_id_type=MESH)

    loads[0].wait()
    p2[...] = jnp.zeros_like(p2)
    p2[:, 0:32] = (pv[0:32, 0:128] + pv[0:32, 128:256]).T
    loads[2].wait()
    tt[...] = tv[...].T
    for b in range(2):
        nothing = jnp.zeros((128, 128), BF16)
        for h in range(2):
            empty = slice(512 * h + 256 * b + 128, 512 * h + 256 * b + 256)
            w_hi[b, empty, 0:128] = nothing
            w_lo[b, empty, 0:128] = nothing
    loads[1].wait()
    loads[3].wait()
    pl.semaphore_wait(barrier, jnp.where(row != z, 24, 23))

    def to_transposed():
        return remote(pv.at[pl.ds(0, 32)], pz.at[k, z], z_s, z_r, (z, 2 * row + k))

    @pl.when(row != z)
    def _():
        to_transposed().start()

    @pl.when(row == z)
    def _():
        pltpu.make_async_copy(pv.at[pl.ds(0, 32)], pz.at[k, z], z_r).start()

    def stride4(d):
        return remote(pv, pr.at[w, k, q], a_s.at[d], a_r.at[d], along(4 * d))

    def to_group(back):
        at = lax.rem(q + 4 - back, 4)
        src, dst = pr.at[w, k, at] if back else pv, pr.at[w, k, at]
        low = at < 2
        return [
            remote(src, dst, b_s.at[back, 2], b_r.at[jnp.where(low, 2, 3)], along(jnp.where(low, 2, -2))),
            remote(src, dst, b_s.at[back, 0], b_r.at[0], along(1)),
            remote(src, dst, b_s.at[back, 1], b_r.at[1], along(-1)),
        ]

    for d in (2, 1, 3):
        stride4(d).start()
    for g in to_group(0):
        g.start()
    pltpu.make_async_copy(pv, pr.at[w, k, q], a_r.at[0]).start()

    def panel_sum(d):
        to = lax.rem(row + d, 16)
        return remote(p2.at[pl.ds(pl.multiple_of(8 * to, 8), 8)], ps1.at[row], p1_s.at[d], p1_r, (to, col))

    @pl.loop(1, 16)
    def _(d):
        panel_sum(d).start()

    ps1[row] = p2[pl.ds(pl.multiple_of(8 * row, 8), 8)]

    share = remote(tt.at[:, other], tx, t_s.at[0], t_r.at[0], sibling)
    share.start()

    arrived(pz.at[k, row], z_r)

    def panel_plane(d):
        return remote(pz.at[k, row], pz.at[k, row], z2_s.at[d], z2_r, (lax.rem(row + d, 16), col))

    @pl.loop(1, 16)
    def _(d):
        panel_plane(d).start()

    arrived(ps1.at[pl.ds(0, 15)], p1_r)
    ps2[...] = jnp.sum(ps1[...], axis=0)

    def sum_transposed():
        return remote(ps2, ps.at[k, z], p3_s, p3_r, (z, 2 * row + k))

    @pl.when(row != z)
    def _():
        sum_transposed().start()

    @pl.when(row == z)
    def _():
        pltpu.make_async_copy(ps2, ps.at[k, z], p3_r).start()

    for d in (1, 3, 2):
        arrived(pr.at[w, k, lax.rem(q + 4 - d, 4)], a_r.at[d])
        for g in to_group(d):
            g.start()
    arrived(pr.at[w, k, q], a_r.at[0])
    first_two, last_two = pr.at[w, k, pl.ds(0, 2)], pr.at[w, k, pl.ds(2, 2)]

    def swap(i, v):
        return remote(pr.at[v, k], pr.at[v, k], x_s.at[i], x_r.at[i], sibling)

    swap(0, w).start()

    share.wait()
    tt[:, half] += tx[...]

    for d in range(16):
        tq[d % 4, d // 4] = tt[8 * d : 8 * d + 8, half]
    left, right, across = lax.rem(w + 3, 4), lax.rem(w + 1, 4), lax.rem(w + 2, 4)
    gather_sums = [
        remote(tq.at[left], ta.at[0], ta_s.at[0], ta_r.at[0], along(-1)),
        remote(tq.at[right], ta.at[1], ta_s.at[1], ta_r.at[1], along(1)),
        remote(tq.at[across, pl.ds(0, 2)], ta.at[2, pl.ds(0, 2)], ta_s.at[2], ta_r.at[2], along(2)),
        remote(tq.at[across, pl.ds(2, 2)], ta.at[2, pl.ds(2, 2)], ta_s.at[3], ta_r.at[3], along(-2)),
    ]
    for g in gather_sums:
        g.start()

    arrived(pr.at[left, k], b_r.at[0])
    swap(1, left).start()
    arrived(pr.at[right, k], b_r.at[1])
    swap(2, right).start()
    arrived(first_two, b_r.at[2])
    arrived(last_two, b_r.at[3])
    swap(3, across).start()

    place = ((y, x), (x, y))
    parity = (k, 1 - k)

    def device(h, o, i):
        return (4 * i + o if h == 0 else 4 * o + i, col)

    def near(h, d):
        o, i = place[h]
        ref = inv.at[h, o, i]
        return remote(ref, ref, near_s.at[h, d - 1], near_r.at[h, d - 1], device(h, o, lax.rem(i + d, 4)))

    def far(h, back, d):
        o, i = place[h]
        ref = inv.at[h, o, lax.rem(i + 4 - back, 4)]
        return remote(ref, ref, far_s.at[h, back, d - 1], far_r.at[h], device(h, lax.rem(o + d, 4), i))

    def pack(h):
        o, i = place[h]
        for n in range(4):
            for g in range(n + 1):
                inv[h, o, i, FIRST[n] + g] = pr[lax.rem(n + 4 - y, 4), parity[h], g, 32:40, half]
        for d in (2, 1, 3):
            near(h, d).start()
        for d in (2, 1, 3):
            far(h, 0, d).start()

    pack(0)
    arrived(ps.at[k, row], p3_r)

    def sum_plane(d):
        return remote(ps.at[k, row], ps.at[k, row], p4_s.at[d], p4_r, (lax.rem(row + d, 16), col))

    @pl.loop(1, 16)
    def _(d):
        sum_plane(d).start()

    for i, v in enumerate((w, left, right, across)):
        arrived(pr.at[v, 1 - k], x_r.at[i])
    pack(1)

    def forward(h, d):
        o, i = place[h]
        arrived(inv.at[h, o, lax.rem(i + 4 - d, 4)], near_r.at[h, d - 1])
        for e in (2, 1, 3):
            far(h, d, e).start()

    for d in (1, 3, 2):
        forward(0, d)
    for d in (1, 3, 2):
        forward(1, d)

    for i, g in enumerate(gather_sums):
        arrived((ta.at[i] if i < 2 else ta.at[2, pl.ds(2 * i - 4, 2)]), ta_r.at[i])
    tb[...] = tq[w] + ta[0] + ta[1] + ta[2]

    def block_sum(d):
        return remote(tb.at[lax.rem(q + d, 4)], tc.at[q], tc_s.at[d], tc_r, along(4 * d))

    for d in (2, 1, 3):
        block_sum(d).start()
    tc[q] = tb[q]

    arrived(pz.at[k, pl.ds(0, 15)], z2_r)
    swap_z = remote(pz.at[k], pz.at[k], x_s.at[4], x_r.at[4], sibling)
    swap_z.start()
    arrived(ps.at[k, pl.ds(0, 15)], p4_r)
    swap_s = remote(ps.at[k], ps.at[k], x_s.at[5], x_r.at[5], sibling)
    swap_s.start()

    for i, v in enumerate((w, left, right, across)):
        swap(i, v).wait_send()
    for m in range(8):
        parts = [pr[v, parity[m // 4], m % 4, 0:32] for v in range(4)]
        at = slice(128 * m, 128 * m + 128)
        p_hi[0:256, at], p_lo[0:256, at] = split(jnp.concatenate(parts, axis=0).T)
    arrived(pz.at[1 - k], x_r.at[4])
    for m in range(8):
        parts = [pz[parity[m // 4], 4 * (m % 4) + v] for v in range(4)]
        at = slice(128 * m, 128 * m + 128)
        p_hi[256:512, at], p_lo[256:512, at] = split(jnp.concatenate(parts, axis=0).T)
    arrived(ps.at[1 - k], x_r.at[5])
    for m in range(8):
        parts = jnp.concatenate([ps[parity[m // 4], 4 * (m % 4) + v][:, 0:32] for v in range(4)], axis=1)
        at = slice(128 * m, 128 * m + 128)
        p_hi[512:528, at], p_lo[512:528, at] = split(jnp.concatenate([parts, jnp.zeros_like(parts)], axis=0))

    arrived(tc.at[pl.ds(0, 3)], tc_r)
    fin[...] = jnp.sum(tc[...], axis=0)
    last = remote(fin, fx, t_s.at[1], t_r.at[1], sibling)
    last.start()

    def put(at, rows, c_rows, s_rows):
        lr_hi[:, at], lr_lo[:, at] = split(rows)
        high, low = split(jnp.concatenate([c_rows, s_rows, jnp.zeros_like(s_rows)], axis=0))
        lc_hi[:, at], lc_lo[:, at] = high, low

    def give(b):
        return remote(gb.at[b], rb.at[b], l_s.at[b], l_r.at[b], sibling)

    blocks = [None, None]
    for h in range(2):
        arrived(inv.at[h, pl.ds(0, 3)], far_r.at[h])
        for b in range(2):
            for e in range(2):
                n = 2 * b + e
                for g in range(n + 1):
                    for v in range(4):
                        sy, at = (n - v) % 4, 512 * h + 32 * (4 * g + v)
                        tiles = [inv[h, sy, sx, FIRST[n] + g] if h == 0 else inv[h, sx, sy, FIRST[n] + g] for sx in range(4)]
                        high, low = split(jnp.concatenate(tiles, axis=0))
                        w_hi[b, at : at + 32, 128 * e : 128 * e + 128] = high
                        w_lo[b, at : at + 32, 128 * e : 128 * e + 128] = low
            deep = slice(512 * h, 512 * h + 256 * (b + 1))
            part = dot3((p_hi[:, deep], p_lo[:, deep]), (w_hi[b, deep, :], w_lo[b, deep, :]), ((1,), (0,)))
            if h == 0:
                part_0[b] = part
            else:
                blocks[b] = part
    for b in range(2):
        block = part_0[b] + blocks[b]
        one, two = block[256:384], block[384:512]
        gb[b, 0:256] = block[0:256]
        gb[b, 256:384] = jnp.where(even, two, one)
        gb[b, 384:392] = block[512:520]
        give(b).start()
        put(slice(512 * b, 512 * b + 256), block[0:256], jnp.where(even, one, two), block[512:520])

    for b in range(2):
        arrived(rb.at[b], l_r.at[b])
        put(slice(512 * b + 256, 512 * b + 512), rb[b, 0:256], rb[b, 256:384], rb[b, 384:392])
    product = dot3((lr_hi[...], lr_lo[...]), (lc_hi[...], lc_lo[...]), ((1,), (1,)))
    u_out[...] = tv[...] - product[:, 0:128]
    correction = product[:, 128:136].T
    correction = jnp.where(even, correction[0:4], correction[4:8])
    last.wait()
    mine, theirs = fin[...], fx[...]
    sums = jnp.concatenate([jnp.where(even, mine, theirs), jnp.where(even, theirs, mine)], axis=1)
    c_out[...] = cv[...] - correction
    e_out[...] = jnp.where(even, sums[0:4], sums[4:8]) - correction

    @pl.when(row != z)
    def _():
        to_transposed().wait_send()
        sum_transposed().wait_send()

    for d in (1, 2, 3):
        stride4(d).wait_send()
        block_sum(d).wait_send()

    for g in gather_sums + [g for back in range(4) for g in to_group(back)]:
        g.wait_send()
    swap_z.wait_send()
    swap_s.wait_send()
    for b in range(2):
        give(b).wait_send()
    for h in range(2):
        for d in (1, 2, 3):
            near(h, d).wait_send()
            for back in range(4):
                far(h, back, d).wait_send()

    @pl.loop(1, 16)
    def _(d):
        panel_plane(d).wait_send()
        panel_sum(d).wait_send()
        sum_plane(d).wait_send()


def on_device(trailing, panel_block, inverse, checksum):
    vmem = pl.BlockSpec(memory_space=pltpu.VMEM)
    dma = pltpu.SemaphoreType.DMA
    updated, checksum_new, reencoded = pl.pallas_call(
        kernel,
        out_shape=(
            jax.ShapeDtypeStruct((256, 128), F32),
            jax.ShapeDtypeStruct((4, 256), F32),
            jax.ShapeDtypeStruct((4, 256), F32),
        ),
        in_specs=[pl.BlockSpec(memory_space=pltpu.HBM)] * 4,
        out_specs=(vmem,) * 3,
        scratch_shapes=[
            pltpu.VMEM((256, 128), F32),
            pltpu.VMEM((40, 256), F32),
            pltpu.VMEM((4, 256), F32),
            pltpu.VMEM((2, 4, 4, 10, 8, 128), F32),
            pltpu.VMEM((4, 2, 4, 40, 256), F32),
            pltpu.VMEM((2, 16, 32, 256), F32),
            pltpu.VMEM((128, 128), F32),
            pltpu.VMEM((16, 8, 128), F32),
            pltpu.VMEM((8, 128), F32),
            pltpu.VMEM((2, 16, 8, 128), F32),
            pltpu.VMEM((128, 256), F32),
            pltpu.VMEM((128, 128), F32),
            pltpu.VMEM((4, 4, 8, 128), F32),
            pltpu.VMEM((3, 4, 8, 128), F32),
            pltpu.VMEM((4, 8, 128), F32),
            pltpu.VMEM((4, 8, 128), F32),
            pltpu.VMEM((8, 128), F32),
            pltpu.VMEM((8, 128), F32),
            pltpu.VMEM((2, 392, 256), F32),
            pltpu.VMEM((2, 392, 256), F32),
            pltpu.VMEM((2, 528, 256), F32),
            pltpu.VMEM((528, 1024), BF16),
            pltpu.VMEM((528, 1024), BF16),
            pltpu.VMEM((2, 1024, 256), BF16),
            pltpu.VMEM((2, 1024, 256), BF16),
            pltpu.VMEM((256, 1024), BF16),
            pltpu.VMEM((256, 1024), BF16),
            pltpu.VMEM((144, 1024), BF16),
            pltpu.VMEM((144, 1024), BF16),
            dma((4,)), dma((2, 3)), dma((2, 3)), dma((2, 4, 3)), dma((2,)),
            dma((4,)), dma((4,)), dma((4, 3)), dma((4,)), dma((6,)), dma((6,)),
            dma, dma, dma((16,)), dma, dma((16,)), dma, dma, dma, dma((16,)), dma,
            dma((2,)), dma((2,)), dma((4,)), dma((4,)), dma((4,)), dma, dma((2,)), dma((2,)),
        ],
        compiler_params=pltpu.CompilerParams(
            collective_id=0, has_side_effects=True, vmem_limit_bytes=62 * 1024 * 1024
        ),
    )(trailing, panel_block.T, inverse.T, checksum.T)
    return updated, checksum_new.T, reencoded.T


def solution(mesh):
    in_specs = (P("row", "col"), P("row", "col"), P(None, "col"), P("row", "col"))
    out_specs = (P("row", "col"), P("row", "col"), P("row", "col"))
    return jax.shard_map(
        on_device, mesh=mesh, in_specs=in_specs, out_specs=out_specs, check_vma=False
    )
```

```python
import jax
import jax.numpy as jnp
from jax import lax
from jax.experimental import pallas as pl
from jax.experimental.pallas import tpu as pltpu
from jax.sharding import PartitionSpec as P

F32, BF16 = jnp.float32, jnp.bfloat16
MESH = pl.DeviceIdType.MESH
FIRST = (0, 1, 3, 6)


def remote(src, dst, send_sem, recv_sem, device):
    return pltpu.make_async_remote_copy(
        src_ref=src,
        dst_ref=dst,
        send_sem=send_sem,
        recv_sem=recv_sem,
        device_id=device,
        device_id_type=MESH,
    )


def arrived(ref, sem):
    pltpu.make_async_copy(ref, ref, sem).wait()


def split(value):
    high = value.astype(BF16)
    return high, (value - high.astype(F32)).astype(BF16)


def dot3(a, b, dims):
    def one(u, v):
        return lax.dot_general(u, v, (dims, ((), ())), preferred_element_type=F32)

    return one(a[0], b[0]) + (one(a[0], b[1]) + one(a[1], b[0]))


def kernel(
    t_ref, p_ref, i_ref, c_ref, u_out, c_out, e_out,
    tv, pv, cv, inv, pr, pz, p2, ps1, ps2, ps, tt, tx, tq, ta, tb, tc, fin, fx, gb, rb, part_0,
    p_hi, p_lo, w_hi, w_lo, lr_hi, lr_lo, lc_hi, lc_lo,
    in_s, near_s, near_r, far_s, far_r, a_s, a_r, b_s, b_r, x_s, x_r,
    z_s, z_r, z2_s, z2_r, p1_s, p1_r, p3_s, p3_r, p4_s, p4_r, t_s, t_r, ta_s, ta_r, tc_s, tc_r, l_s, l_r,
):
    row, col = lax.axis_index("row"), lax.axis_index("col")
    z, k = col // 2, lax.rem(col, 2)
    x, y = row // 4, lax.rem(row, 4)
    q, w = z // 4, lax.rem(z, 4)
    p = lax.rem(y + w, 4)
    even = k == 0
    tile_rows = pl.ds(pl.multiple_of(8 * x, 8), 8)
    loads = [
        pltpu.make_async_copy(p_ref, pv.at[pl.ds(0, 32)], in_s.at[0]),
        pltpu.make_async_copy(i_ref.at[tile_rows, pl.ds(pl.multiple_of(256 * p, 256), 256)], pv.at[pl.ds(32, 8)], in_s.at[1]),
        pltpu.make_async_copy(t_ref, tv, in_s.at[2]),
        pltpu.make_async_copy(c_ref, cv, in_s.at[3]),
    ]
    for load in loads:
        load.start()
    sibling = (row, 2 * z + 1 - k)
    half, other = pl.ds(pl.multiple_of(128 * k, 128), 128), pl.ds(pl.multiple_of(128 * (1 - k), 128), 128)

    def along(d):
        return (row, 2 * lax.rem(z + d + 16, 16) + k)

    barrier = pltpu.get_barrier_semaphore()

    for d in (8, 4, -4, 2, -2, 1, -1):
        pl.semaphore_signal(barrier, inc=1, device_id=along(d), device_id_type=MESH)
    pl.semaphore_signal(barrier, inc=1, device_id=sibling, device_id_type=MESH)

    @pl.loop(1, 16)
    def _(d):
        pl.semaphore_signal(barrier, inc=1, device_id=(lax.rem(row + d, 16), col), device_id_type=MESH)

    @pl.when(row != z)
    def _():
        pl.semaphore_signal(barrier, inc=1, device_id=(z, 2 * row + k), device_id_type=MESH)

    loads[0].wait()
    p2[...] = jnp.zeros_like(p2)
    p2[:, 0:32] = (pv[0:32, 0:128] + pv[0:32, 128:256]).T
    loads[2].wait()
    tt[...] = tv[...].T
    for b in range(2):
        nothing = jnp.zeros((128, 128), BF16)
        for h in range(2):
            empty = slice(512 * h + 256 * b + 128, 512 * h + 256 * b + 256)
            w_hi[b, empty, 0:128] = nothing
            w_lo[b, empty, 0:128] = nothing
    loads[1].wait()
    loads[3].wait()
    pl.semaphore_wait(barrier, jnp.where(row != z, 24, 23))

    def to_transposed():
        return remote(pv.at[pl.ds(0, 32)], pz.at[k, z], z_s, z_r, (z, 2 * row + k))

    @pl.when(row != z)
    def _():
        to_transposed().start()

    @pl.when(row == z)
    def _():
        pltpu.make_async_copy(pv.at[pl.ds(0, 32)], pz.at[k, z], z_r).start()

    def stride4(d):
        return remote(pv, pr.at[w, k, q], a_s.at[d], a_r.at[d], along(4 * d))

    def to_group(back):
        at = lax.rem(q + 4 - back, 4)
        src, dst = pr.at[w, k, at] if back else pv, pr.at[w, k, at]
        low = at < 2
        return [
            remote(src, dst, b_s.at[back, 2], b_r.at[jnp.where(low, 2, 3)], along(jnp.where(low, 2, -2))),
            remote(src, dst, b_s.at[back, 0], b_r.at[0], along(1)),
            remote(src, dst, b_s.at[back, 1], b_r.at[1], along(-1)),
        ]

    for d in (2, 1, 3):
        stride4(d).start()
    for g in to_group(0):
        g.start()
    pltpu.make_async_copy(pv, pr.at[w, k, q], a_r.at[0]).start()

    def panel_sum(d):
        to = lax.rem(row + d, 16)
        return remote(p2.at[pl.ds(pl.multiple_of(8 * to, 8), 8)], ps1.at[row], p1_s.at[d], p1_r, (to, col))

    @pl.loop(1, 16)
    def _(d):
        panel_sum(d).start()

    ps1[row] = p2[pl.ds(pl.multiple_of(8 * row, 8), 8)]

    share = remote(tt.at[:, other], tx, t_s.at[0], t_r.at[0], sibling)
    share.start()

    arrived(pz.at[k, row], z_r)

    def panel_plane(d):
        return remote(pz.at[k, row], pz.at[k, row], z2_s.at[d], z2_r, (lax.rem(row + d, 16), col))

    @pl.loop(1, 16)
    def _(d):
        panel_plane(d).start()

    arrived(ps1.at[pl.ds(0, 15)], p1_r)
    ps2[...] = jnp.sum(ps1[...], axis=0)

    def sum_transposed():
        return remote(ps2, ps.at[k, z], p3_s, p3_r, (z, 2 * row + k))

    @pl.when(row != z)
    def _():
        sum_transposed().start()

    @pl.when(row == z)
    def _():
        pltpu.make_async_copy(ps2, ps.at[k, z], p3_r).start()

    for d in (1, 3, 2):
        arrived(pr.at[w, k, lax.rem(q + 4 - d, 4)], a_r.at[d])
        for g in to_group(d):
            g.start()
    arrived(pr.at[w, k, q], a_r.at[0])
    first_two, last_two = pr.at[w, k, pl.ds(0, 2)], pr.at[w, k, pl.ds(2, 2)]

    def swap(i, v):
        return remote(pr.at[v, k], pr.at[v, k], x_s.at[i], x_r.at[i], sibling)

    swap(0, w).start()

    share.wait()
    tt[:, half] += tx[...]

    for d in range(16):
        tq[d % 4, d // 4] = tt[8 * d : 8 * d + 8, half]
    left, right, across = lax.rem(w + 3, 4), lax.rem(w + 1, 4), lax.rem(w + 2, 4)
    gather_sums = [
        remote(tq.at[left], ta.at[0], ta_s.at[0], ta_r.at[0], along(-1)),
        remote(tq.at[right], ta.at[1], ta_s.at[1], ta_r.at[1], along(1)),
        remote(tq.at[across, pl.ds(0, 2)], ta.at[2, pl.ds(0, 2)], ta_s.at[2], ta_r.at[2], along(2)),
        remote(tq.at[across, pl.ds(2, 2)], ta.at[2, pl.ds(2, 2)], ta_s.at[3], ta_r.at[3], along(-2)),
    ]
    for g in gather_sums:
        g.start()

    arrived(pr.at[left, k], b_r.at[0])
    swap(1, left).start()
    arrived(pr.at[right, k], b_r.at[1])
    swap(2, right).start()
    arrived(first_two, b_r.at[2])
    arrived(last_two, b_r.at[3])
    swap(3, across).start()

    place = ((y, x), (x, y))
    parity = (k, 1 - k)

    def device(h, o, i):
        return (4 * i + o if h == 0 else 4 * o + i, col)

    def near(h, d):
        o, i = place[h]
        ref = inv.at[h, o, i]
        return remote(ref, ref, near_s.at[h, d - 1], near_r.at[h, d - 1], device(h, o, lax.rem(i + d, 4)))

    def far(h, back, d):
        o, i = place[h]
        ref = inv.at[h, o, lax.rem(i + 4 - back, 4)]
        return remote(ref, ref, far_s.at[h, back, d - 1], far_r.at[h], device(h, lax.rem(o + d, 4), i))

    def pack(h):
        o, i = place[h]
        for n in range(4):
            for g in range(n + 1):
                inv[h, o, i, FIRST[n] + g] = pr[lax.rem(n + 4 - y, 4), parity[h], g, 32:40, half]
        for d in (2, 1, 3):
            near(h, d).start()
        for d in (2, 1, 3):
            far(h, 0, d).start()

    pack(0)
    arrived(ps.at[k, row], p3_r)

    def sum_plane(d):
        return remote(ps.at[k, row], ps.at[k, row], p4_s.at[d], p4_r, (lax.rem(row + d, 16), col))

    @pl.loop(1, 16)
    def _(d):
        sum_plane(d).start()

    for i, v in enumerate((w, left, right, across)):
        arrived(pr.at[v, 1 - k], x_r.at[i])
    pack(1)

    def forward(h, d):
        o, i = place[h]
        arrived(inv.at[h, o, lax.rem(i + 4 - d, 4)], near_r.at[h, d - 1])
        for e in (2, 1, 3):
            far(h, d, e).start()

    for d in (1, 3, 2):
        forward(0, d)
    for d in (1, 3, 2):
        forward(1, d)

    for i, g in enumerate(gather_sums):
        arrived((ta.at[i] if i < 2 else ta.at[2, pl.ds(2 * i - 4, 2)]), ta_r.at[i])
    tb[...] = tq[w] + ta[0] + ta[1] + ta[2]

    def block_sum(d):
        return remote(tb.at[lax.rem(q + d, 4)], tc.at[q], tc_s.at[d], tc_r, along(4 * d))

    for d in (2, 1, 3):
        block_sum(d).start()
    tc[q] = tb[q]

    arrived(pz.at[k, pl.ds(0, 15)], z2_r)
    swap_z = remote(pz.at[k], pz.at[k], x_s.at[4], x_r.at[4], sibling)
    swap_z.start()
    arrived(ps.at[k, pl.ds(0, 15)], p4_r)
    swap_s = remote(ps.at[k], ps.at[k], x_s.at[5], x_r.at[5], sibling)
    swap_s.start()

    for i, v in enumerate((w, left, right, across)):
        swap(i, v).wait_send()
    for m in range(8):
        parts = [pr[v, parity[m // 4], m % 4, 0:32] for v in range(4)]
        at = slice(128 * m, 128 * m + 128)
        p_hi[0:256, at], p_lo[0:256, at] = split(jnp.concatenate(parts, axis=0).T)
    arrived(pz.at[1 - k], x_r.at[4])
    for m in range(8):
        parts = [pz[parity[m // 4], 4 * (m % 4) + v] for v in range(4)]
        at = slice(128 * m, 128 * m + 128)
        p_hi[256:512, at], p_lo[256:512, at] = split(jnp.concatenate(parts, axis=0).T)
    arrived(ps.at[1 - k], x_r.at[5])
    for m in range(8):
        parts = jnp.concatenate([ps[parity[m // 4], 4 * (m % 4) + v][:, 0:32] for v in range(4)], axis=1)
        at = slice(128 * m, 128 * m + 128)
        p_hi[512:528, at], p_lo[512:528, at] = split(jnp.concatenate([parts, jnp.zeros_like(parts)], axis=0))

    arrived(tc.at[pl.ds(0, 3)], tc_r)
    fin[...] = jnp.sum(tc[...], axis=0)
    last = remote(fin, fx, t_s.at[1], t_r.at[1], sibling)
    last.start()

    def put(at, rows, c_rows, s_rows):
        lr_hi[:, at], lr_lo[:, at] = split(rows)
        high, low = split(jnp.concatenate([c_rows, s_rows, jnp.zeros_like(s_rows)], axis=0))
        lc_hi[:, at], lc_lo[:, at] = high, low

    def give(b):
        return remote(gb.at[b], rb.at[b], l_s.at[b], l_r.at[b], sibling)

    blocks = [None, None]
    for h in range(2):
        arrived(inv.at[h, pl.ds(0, 3)], far_r.at[h])
        for b in range(2):
            for e in range(2):
                n = 2 * b + e
                for g in range(n + 1):
                    for v in range(4):
                        sy, at = (n - v) % 4, 512 * h + 32 * (4 * g + v)
                        tiles = [inv[h, sy, sx, FIRST[n] + g] if h == 0 else inv[h, sx, sy, FIRST[n] + g] for sx in range(4)]
                        high, low = split(jnp.concatenate(tiles, axis=0))
                        w_hi[b, at : at + 32, 128 * e : 128 * e + 128] = high
                        w_lo[b, at : at + 32, 128 * e : 128 * e + 128] = low
            deep = slice(512 * h, 512 * h + 256 * (b + 1))
            part = dot3((p_hi[:, deep], p_lo[:, deep]), (w_hi[b, deep, :], w_lo[b, deep, :]), ((1,), (0,)))
            if h == 0:
                part_0[b] = part
            else:
                blocks[b] = part
    for b in range(2):
        block = part_0[b] + blocks[b]
        one, two = block[256:384], block[384:512]
        gb[b, 0:256] = block[0:256]
        gb[b, 256:384] = jnp.where(even, two, one)
        gb[b, 384:392] = block[512:520]
        give(b).start()
        put(slice(512 * b, 512 * b + 256), block[0:256], jnp.where(even, one, two), block[512:520])

    for b in range(2):
        arrived(rb.at[b], l_r.at[b])
        put(slice(512 * b + 256, 512 * b + 512), rb[b, 0:256], rb[b, 256:384], rb[b, 384:392])
    product = dot3((lr_hi[...], lr_lo[...]), (lc_hi[...], lc_lo[...]), ((1,), (1,)))
    u_out[...] = tv[...] - product[:, 0:128]
    correction = product[:, 128:136].T
    correction = jnp.where(even, correction[0:4], correction[4:8])
    last.wait()
    mine, theirs = fin[...], fx[...]
    sums = jnp.concatenate([jnp.where(even, mine, theirs), jnp.where(even, theirs, mine)], axis=1)
    c_out[...] = cv[...] - correction
    e_out[...] = jnp.where(even, sums[0:4], sums[4:8]) - correction

    @pl.when(row != z)
    def _():
        to_transposed().wait_send()
        sum_transposed().wait_send()

    for d in (1, 2, 3):
        stride4(d).wait_send()
        block_sum(d).wait_send()

    for g in gather_sums + [g for back in range(4) for g in to_group(back)]:
        g.wait_send()
    swap_z.wait_send()
    swap_s.wait_send()
    for b in range(2):
        give(b).wait_send()
    for h in range(2):
        for d in (1, 2, 3):
            near(h, d).wait_send()
            for back in range(4):
                far(h, back, d).wait_send()

    @pl.loop(1, 16)
    def _(d):
        panel_plane(d).wait_send()
        panel_sum(d).wait_send()
        sum_plane(d).wait_send()


def on_device(trailing, panel_block, inverse, checksum):
    vmem = pl.BlockSpec(memory_space=pltpu.VMEM)
    dma = pltpu.SemaphoreType.DMA
    updated, checksum_new, reencoded = pl.pallas_call(
        kernel,
        out_shape=(
            jax.ShapeDtypeStruct((256, 128), F32),
            jax.ShapeDtypeStruct((4, 256), F32),
            jax.ShapeDtypeStruct((4, 256), F32),
        ),
        in_specs=[pl.BlockSpec(memory_space=pltpu.HBM)] * 4,
        out_specs=(vmem,) * 3,
        scratch_shapes=[
            pltpu.VMEM((256, 128), F32),
            pltpu.VMEM((40, 256), F32),
            pltpu.VMEM((4, 256), F32),
            pltpu.VMEM((2, 4, 4, 10, 8, 128), F32),
            pltpu.VMEM((4, 2, 4, 40, 256), F32),
            pltpu.VMEM((2, 16, 32, 256), F32),
            pltpu.VMEM((128, 128), F32),
            pltpu.VMEM((16, 8, 128), F32),
            pltpu.VMEM((8, 128), F32),
            pltpu.VMEM((2, 16, 8, 128), F32),
            pltpu.VMEM((128, 256), F32),
            pltpu.VMEM((128, 128), F32),
            pltpu.VMEM((4, 4, 8, 128), F32),
            pltpu.VMEM((3, 4, 8, 128), F32),
            pltpu.VMEM((4, 8, 128), F32),
            pltpu.VMEM((4, 8, 128), F32),
            pltpu.VMEM((8, 128), F32),
            pltpu.VMEM((8, 128), F32),
            pltpu.VMEM((2, 392, 256), F32),
            pltpu.VMEM((2, 392, 256), F32),
            pltpu.VMEM((2, 528, 256), F32),
            pltpu.VMEM((528, 1024), BF16),
            pltpu.VMEM((528, 1024), BF16),
            pltpu.VMEM((2, 1024, 256), BF16),
            pltpu.VMEM((2, 1024, 256), BF16),
            pltpu.VMEM((256, 1024), BF16),
            pltpu.VMEM((256, 1024), BF16),
            pltpu.VMEM((144, 1024), BF16),
            pltpu.VMEM((144, 1024), BF16),
            dma((4,)), dma((2, 3)), dma((2, 3)), dma((2, 4, 3)), dma((2,)),
            dma((4,)), dma((4,)), dma((4, 3)), dma((4,)), dma((6,)), dma((6,)),
            dma, dma, dma((16,)), dma, dma((16,)), dma, dma, dma, dma((16,)), dma,
            dma((2,)), dma((2,)), dma((4,)), dma((4,)), dma((4,)), dma, dma((2,)), dma((2,)),
        ],
        compiler_params=pltpu.CompilerParams(
            collective_id=0, has_side_effects=True, vmem_limit_bytes=48 * 1024 * 1024
        ),
    )(*(pltpu.with_memory_space_constraint(v, pltpu.HBM) for v in (trailing, panel_block.T, inverse.T, checksum.T)))
    return updated, checksum_new.T, reencoded.T


def solution(mesh):
    in_specs = (P("row", "col"), P("row", "col"), P(None, "col"), P("row", "col"))
    out_specs = (P("row", "col"), P("row", "col"), P("row", "col"))
    return jax.shard_map(
        on_device, mesh=mesh, in_specs=in_specs, out_specs=out_specs, check_vma=False
    )
```

```python
import jax
import jax.numpy as jnp
from jax import lax
from jax.experimental import pallas as pl
from jax.experimental.pallas import tpu as pltpu
from jax.sharding import PartitionSpec as P

F32, BF16 = jnp.float32, jnp.bfloat16
MESH = pl.DeviceIdType.MESH
FIRST = (0, 1, 3, 6)


def remote(src, dst, send_sem, recv_sem, device):
    return pltpu.make_async_remote_copy(
        src_ref=src,
        dst_ref=dst,
        send_sem=send_sem,
        recv_sem=recv_sem,
        device_id=device,
        device_id_type=MESH,
    )


def arrived(ref, sem):
    pltpu.make_async_copy(ref, ref, sem).wait()


def split(value):
    high = value.astype(BF16)
    return high, (value - high.astype(F32)).astype(BF16)


def dot3(a, b, dims):
    def one(u, v):
        return lax.dot_general(u, v, (dims, ((), ())), preferred_element_type=F32)

    return one(a[0], b[0]) + (one(a[0], b[1]) + one(a[1], b[0]))


def kernel(
    t_ref, p_ref, i_ref, c_ref, u_out, c_out, e_out,
    tv, pv, cv, inv, pr, pz, p2, ps1, ps2, ps, tt, tx, tq, ta, tb, tc, fin, fx, gb, rb, part_0,
    p_hi, p_lo, w_hi, w_lo, lr_hi, lr_lo, lc_hi, lc_lo,
    in_s, near_s, near_r, far_s, far_r, a_s, a_r, b_s, b_r, x_s, x_r,
    z_s, z_r, z2_s, z2_r, p1_s, p1_r, p3_s, p3_r, p4_s, p4_r, t_s, t_r, ta_s, ta_r, tc_s, tc_r, l_s, l_r,
):
    row, col = lax.axis_index("row"), lax.axis_index("col")
    z, k = col // 2, lax.rem(col, 2)
    x, y = row // 4, lax.rem(row, 4)
    q, w = z // 4, lax.rem(z, 4)
    p = lax.rem(y + w, 4)
    even = k == 0
    tile_rows = pl.ds(pl.multiple_of(8 * x, 8), 8)
    loads = [
        pltpu.make_async_copy(p_ref, pv.at[pl.ds(0, 32)], in_s.at[0]),
        pltpu.make_async_copy(i_ref.at[tile_rows, pl.ds(pl.multiple_of(256 * p, 256), 256)], pv.at[pl.ds(32, 8)], in_s.at[1]),
        pltpu.make_async_copy(t_ref, tv, in_s.at[2]),
        pltpu.make_async_copy(c_ref, cv, in_s.at[3]),
    ]
    for load in loads:
        load.start()
    sibling = (row, 2 * z + 1 - k)
    half, other = pl.ds(pl.multiple_of(128 * k, 128), 128), pl.ds(pl.multiple_of(128 * (1 - k), 128), 128)

    def along(d):
        return (row, 2 * lax.rem(z + d + 16, 16) + k)

    barrier = pltpu.get_barrier_semaphore()

    for d in (8, 4, -4, 2, -2, 1, -1):
        pl.semaphore_signal(barrier, inc=1, device_id=along(d), device_id_type=MESH)
    pl.semaphore_signal(barrier, inc=1, device_id=sibling, device_id_type=MESH)

    @pl.loop(1, 16)
    def _(d):
        pl.semaphore_signal(barrier, inc=1, device_id=(lax.rem(row + d, 16), col), device_id_type=MESH)

    @pl.when(row != z)
    def _():
        pl.semaphore_signal(barrier, inc=1, device_id=(z, 2 * row + k), device_id_type=MESH)

    loads[0].wait()
    p2[...] = jnp.zeros_like(p2)
    p2[:, 0:32] = (pv[0:32, 0:128] + pv[0:32, 128:256]).T
    loads[2].wait()
    tt[...] = tv[...].T
    for b in range(2):
        nothing = jnp.zeros((128, 128), BF16)
        for h in range(2):
            empty = slice(512 * h + 256 * b + 128, 512 * h + 256 * b + 256)
            w_hi[b, empty, 0:128] = nothing
            w_lo[b, empty, 0:128] = nothing
    loads[1].wait()
    loads[3].wait()
    pl.semaphore_wait(barrier, jnp.where(row != z, 24, 23))

    def to_transposed():
        return remote(pv.at[pl.ds(0, 32)], pz.at[k, z], z_s, z_r, (z, 2 * row + k))

    @pl.when(row != z)
    def _():
        to_transposed().start()

    @pl.when(row == z)
    def _():
        pltpu.make_async_copy(pv.at[pl.ds(0, 32)], pz.at[k, z], z_r).start()

    def stride4(d):
        return remote(pv, pr.at[w, k, q], a_s.at[d], a_r.at[d], along(4 * d))

    def to_group(back):
        at = lax.rem(q + 4 - back, 4)
        src, dst = pr.at[w, k, at] if back else pv, pr.at[w, k, at]
        low = at < 2
        return [
            remote(src, dst, b_s.at[back, 2], b_r.at[jnp.where(low, 2, 3)], along(jnp.where(low, 2, -2))),
            remote(src, dst, b_s.at[back, 0], b_r.at[0], along(1)),
            remote(src, dst, b_s.at[back, 1], b_r.at[1], along(-1)),
        ]

    for d in (2, 1, 3):
        stride4(d).start()
    for g in to_group(0):
        g.start()
    pltpu.make_async_copy(pv, pr.at[w, k, q], a_r.at[0]).start()

    def panel_sum(d):
        to = lax.rem(row + d, 16)
        return remote(p2.at[pl.ds(pl.multiple_of(8 * to, 8), 8)], ps1.at[row], p1_s.at[d], p1_r, (to, col))

    @pl.loop(1, 16)
    def _(d):
        panel_sum(d).start()

    ps1[row] = p2[pl.ds(pl.multiple_of(8 * row, 8), 8)]

    share = remote(tt.at[:, other], tx, t_s.at[0], t_r.at[0], sibling)
    share.start()

    arrived(pz.at[k, row], z_r)

    def panel_plane(d):
        return remote(pz.at[k, row], pz.at[k, row], z2_s.at[d], z2_r, (lax.rem(row + d, 16), col))

    @pl.loop(1, 16)
    def _(d):
        panel_plane(d).start()

    arrived(ps1.at[pl.ds(0, 15)], p1_r)
    ps2[...] = jnp.sum(ps1[...], axis=0)

    def sum_transposed():
        return remote(ps2, ps.at[k, z], p3_s, p3_r, (z, 2 * row + k))

    @pl.when(row != z)
    def _():
        sum_transposed().start()

    @pl.when(row == z)
    def _():
        pltpu.make_async_copy(ps2, ps.at[k, z], p3_r).start()

    for d in (1, 3, 2):
        arrived(pr.at[w, k, lax.rem(q + 4 - d, 4)], a_r.at[d])
        for g in to_group(d):
            g.start()
    arrived(pr.at[w, k, q], a_r.at[0])
    first_two, last_two = pr.at[w, k, pl.ds(0, 2)], pr.at[w, k, pl.ds(2, 2)]

    def swap(i, v):
        return remote(pr.at[v, k], pr.at[v, k], x_s.at[i], x_r.at[i], sibling)

    swap(0, w).start()

    share.wait()
    tt[:, half] += tx[...]

    for d in range(16):
        tq[d % 4, d // 4] = tt[8 * d : 8 * d + 8, half]
    left, right, across = lax.rem(w + 3, 4), lax.rem(w + 1, 4), lax.rem(w + 2, 4)
    gather_sums = [
        remote(tq.at[left], ta.at[0], ta_s.at[0], ta_r.at[0], along(-1)),
        remote(tq.at[right], ta.at[1], ta_s.at[1], ta_r.at[1], along(1)),
        remote(tq.at[across, pl.ds(0, 2)], ta.at[2, pl.ds(0, 2)], ta_s.at[2], ta_r.at[2], along(2)),
        remote(tq.at[across, pl.ds(2, 2)], ta.at[2, pl.ds(2, 2)], ta_s.at[3], ta_r.at[3], along(-2)),
    ]
    for g in gather_sums:
        g.start()

    arrived(pr.at[left, k], b_r.at[0])
    swap(1, left).start()
    arrived(pr.at[right, k], b_r.at[1])
    swap(2, right).start()
    arrived(first_two, b_r.at[2])
    arrived(last_two, b_r.at[3])
    swap(3, across).start()

    place = ((y, x), (x, y))
    parity = (k, 1 - k)

    def device(h, o, i):
        return (4 * i + o if h == 0 else 4 * o + i, col)

    def near(h, d):
        o, i = place[h]
        ref = inv.at[h, o, i]
        return remote(ref, ref, near_s.at[h, d - 1], near_r.at[h, d - 1], device(h, o, lax.rem(i + d, 4)))

    def far(h, back, d):
        o, i = place[h]
        ref = inv.at[h, o, lax.rem(i + 4 - back, 4)]
        return remote(ref, ref, far_s.at[h, back, d - 1], far_r.at[h], device(h, lax.rem(o + d, 4), i))

    def pack(h):
        o, i = place[h]
        for n in range(4):
            for g in range(n + 1):
                inv[h, o, i, FIRST[n] + g] = pr[lax.rem(n + 4 - y, 4), parity[h], g, 32:40, half]
        for d in (2, 1, 3):
            near(h, d).start()
        for d in (2, 1, 3):
            far(h, 0, d).start()

    pack(0)
    arrived(ps.at[k, row], p3_r)

    def sum_plane(d):
        return remote(ps.at[k, row], ps.at[k, row], p4_s.at[d], p4_r, (lax.rem(row + d, 16), col))

    @pl.loop(1, 16)
    def _(d):
        sum_plane(d).start()

    for i, v in enumerate((w, left, right, across)):
        arrived(pr.at[v, 1 - k], x_r.at[i])
    pack(1)

    def forward(h, d):
        o, i = place[h]
        arrived(inv.at[h, o, lax.rem(i + 4 - d, 4)], near_r.at[h, d - 1])
        for e in (2, 1, 3):
            far(h, d, e).start()

    for d in (1, 3, 2):
        forward(0, d)
    for d in (1, 3, 2):
        forward(1, d)

    for i, g in enumerate(gather_sums):
        arrived((ta.at[i] if i < 2 else ta.at[2, pl.ds(2 * i - 4, 2)]), ta_r.at[i])
    tb[...] = tq[w] + ta[0] + ta[1] + ta[2]

    def block_sum(d):
        return remote(tb.at[lax.rem(q + d, 4)], tc.at[q], tc_s.at[d], tc_r, along(4 * d))

    for d in (2, 1, 3):
        block_sum(d).start()
    tc[q] = tb[q]

    arrived(pz.at[k, pl.ds(0, 15)], z2_r)
    swap_z = remote(pz.at[k], pz.at[k], x_s.at[4], x_r.at[4], sibling)
    swap_z.start()
    arrived(ps.at[k, pl.ds(0, 15)], p4_r)
    swap_s = remote(ps.at[k], ps.at[k], x_s.at[5], x_r.at[5], sibling)
    swap_s.start()

    for i, v in enumerate((w, left, right, across)):
        swap(i, v).wait_send()
    for m in range(8):
        parts = [pr[v, parity[m // 4], m % 4, 0:32] for v in range(4)]
        at = slice(128 * m, 128 * m + 128)
        p_hi[0:256, at], p_lo[0:256, at] = split(jnp.concatenate(parts, axis=0).T)
    arrived(pz.at[1 - k], x_r.at[4])
    for m in range(8):
        parts = [pz[parity[m // 4], 4 * (m % 4) + v] for v in range(4)]
        at = slice(128 * m, 128 * m + 128)
        p_hi[256:512, at], p_lo[256:512, at] = split(jnp.concatenate(parts, axis=0).T)
    arrived(ps.at[1 - k], x_r.at[5])
    for m in range(8):
        parts = jnp.concatenate([ps[parity[m // 4], 4 * (m % 4) + v][:, 0:32] for v in range(4)], axis=1)
        at = slice(128 * m, 128 * m + 128)
        p_hi[512:528, at], p_lo[512:528, at] = split(jnp.concatenate([parts, jnp.zeros_like(parts)], axis=0))

    arrived(tc.at[pl.ds(0, 3)], tc_r)
    fin[...] = jnp.sum(tc[...], axis=0)
    last = remote(fin, fx, t_s.at[1], t_r.at[1], sibling)
    last.start()

    def put(at, rows, c_rows, s_rows):
        lr_hi[:, at], lr_lo[:, at] = split(rows)
        high, low = split(jnp.concatenate([c_rows, s_rows, jnp.zeros_like(s_rows)], axis=0))
        lc_hi[:, at], lc_lo[:, at] = high, low

    def give(b):
        return remote(gb.at[b], rb.at[b], l_s.at[b], l_r.at[b], sibling)

    for h in range(2):
        arrived(inv.at[h, pl.ds(0, 3)], far_r.at[h])
        for b in range(2):
            for e in range(2):
                n = 2 * b + e
                for g in range(n + 1):
                    for v in range(4):
                        sy, at = (n - v) % 4, 512 * h + 32 * (4 * g + v)
                        tiles = [inv[h, sy, sx, FIRST[n] + g] if h == 0 else inv[h, sx, sy, FIRST[n] + g] for sx in range(4)]
                        high, low = split(jnp.concatenate(tiles, axis=0))
                        w_hi[b, at : at + 32, 128 * e : 128 * e + 128] = high
                        w_lo[b, at : at + 32, 128 * e : 128 * e + 128] = low
            deep = slice(512 * h, 512 * h + 256 * (b + 1))
            part = dot3((p_hi[:, deep], p_lo[:, deep]), (w_hi[b, deep, :], w_lo[b, deep, :]), ((1,), (0,)))
            if h == 0:
                part_0[b] = part
            else:
                block = part_0[b] + part
                one, two = block[256:384], block[384:512]
                gb[b, 0:256] = block[0:256]
                gb[b, 256:384] = jnp.where(even, two, one)
                gb[b, 384:392] = block[512:520]
                give(b).start()
                put(slice(512 * b, 512 * b + 256), block[0:256], jnp.where(even, one, two), block[512:520])

    for b in range(2):
        arrived(rb.at[b], l_r.at[b])
        put(slice(512 * b + 256, 512 * b + 512), rb[b, 0:256], rb[b, 256:384], rb[b, 384:392])
    product = dot3((lr_hi[...], lr_lo[...]), (lc_hi[...], lc_lo[...]), ((1,), (1,)))
    u_out[...] = tv[...] - product[:, 0:128]
    correction = product[:, 128:136].T
    correction = jnp.where(even, correction[0:4], correction[4:8])
    last.wait()
    mine, theirs = fin[...], fx[...]
    sums = jnp.concatenate([jnp.where(even, mine, theirs), jnp.where(even, theirs, mine)], axis=1)
    c_out[...] = cv[...] - correction
    e_out[...] = jnp.where(even, sums[0:4], sums[4:8]) - correction

    @pl.when(row != z)
    def _():
        to_transposed().wait_send()
        sum_transposed().wait_send()

    for d in (1, 2, 3):
        stride4(d).wait_send()
        block_sum(d).wait_send()

    for g in gather_sums + [g for back in range(4) for g in to_group(back)]:
        g.wait_send()
    swap_z.wait_send()
    swap_s.wait_send()
    for b in range(2):
        give(b).wait_send()
    for h in range(2):
        for d in (1, 2, 3):
            near(h, d).wait_send()
            for back in range(4):
                far(h, back, d).wait_send()

    @pl.loop(1, 16)
    def _(d):
        panel_plane(d).wait_send()
        panel_sum(d).wait_send()
        sum_plane(d).wait_send()


def on_device(trailing, panel_block, inverse, checksum):
    vmem = pl.BlockSpec(memory_space=pltpu.VMEM)
    dma = pltpu.SemaphoreType.DMA
    updated, checksum_new, reencoded = pl.pallas_call(
        kernel,
        out_shape=(
            jax.ShapeDtypeStruct((256, 128), F32),
            jax.ShapeDtypeStruct((4, 256), F32),
            jax.ShapeDtypeStruct((4, 256), F32),
        ),
        in_specs=[pl.BlockSpec(memory_space=pltpu.HBM)] * 4,
        out_specs=(vmem,) * 3,
        scratch_shapes=[
            pltpu.VMEM((256, 128), F32),
            pltpu.VMEM((40, 256), F32),
            pltpu.VMEM((4, 256), F32),
            pltpu.VMEM((2, 4, 4, 10, 8, 128), F32),
            pltpu.VMEM((4, 2, 4, 40, 256), F32),
            pltpu.VMEM((2, 16, 32, 256), F32),
            pltpu.VMEM((128, 128), F32),
            pltpu.VMEM((16, 8, 128), F32),
            pltpu.VMEM((8, 128), F32),
            pltpu.VMEM((2, 16, 8, 128), F32),
            pltpu.VMEM((128, 256), F32),
            pltpu.VMEM((128, 128), F32),
            pltpu.VMEM((4, 4, 8, 128), F32),
            pltpu.VMEM((3, 4, 8, 128), F32),
            pltpu.VMEM((4, 8, 128), F32),
            pltpu.VMEM((4, 8, 128), F32),
            pltpu.VMEM((8, 128), F32),
            pltpu.VMEM((8, 128), F32),
            pltpu.VMEM((2, 392, 256), F32),
            pltpu.VMEM((2, 392, 256), F32),
            pltpu.VMEM((2, 528, 256), F32),
            pltpu.VMEM((528, 1024), BF16),
            pltpu.VMEM((528, 1024), BF16),
            pltpu.VMEM((2, 1024, 256), BF16),
            pltpu.VMEM((2, 1024, 256), BF16),
            pltpu.VMEM((256, 1024), BF16),
            pltpu.VMEM((256, 1024), BF16),
            pltpu.VMEM((144, 1024), BF16),
            pltpu.VMEM((144, 1024), BF16),
            dma((4,)), dma((2, 3)), dma((2, 3)), dma((2, 4, 3)), dma((2,)),
            dma((4,)), dma((4,)), dma((4, 3)), dma((4,)), dma((6,)), dma((6,)),
            dma, dma, dma((16,)), dma, dma((16,)), dma, dma, dma, dma((16,)), dma,
            dma((2,)), dma((2,)), dma((4,)), dma((4,)), dma((4,)), dma, dma((2,)), dma((2,)),
        ],
        compiler_params=pltpu.CompilerParams(
            collective_id=0, has_side_effects=True, vmem_limit_bytes=48 * 1024 * 1024
        ),
    )(*(pltpu.with_memory_space_constraint(v, pltpu.HBM) for v in (trailing, panel_block.T, inverse.T, checksum.T)))
    return updated, checksum_new.T, reencoded.T


def solution(mesh):
    in_specs = (P("row", "col"), P("row", "col"), P(None, "col"), P("row", "col"))
    out_specs = (P("row", "col"), P("row", "col"), P("row", "col"))
    return jax.shard_map(
        on_device, mesh=mesh, in_specs=in_specs, out_specs=out_specs, check_vma=False
    )
```
